32 devices in a mesh: row: 8 (over y, x, core), col: 4 (over z).
Axes of the slice: x: 2, y: 2, z: 4, core: 2. Of those that a mesh axis runs over, the one named last changes fastest.
Arguments:
- activations: bfloat16 [384, 49, 512], P(('row', 'col'))
- pre_activation: bfloat16 [384, 49, 1024], P(('row', 'col')), may hold values from -6 to 6
- pooled_grad: float32 [384, 1024], P(('row', 'col')), may hold values from -300 to 300
- weights: bfloat16 [512, 1024], replicated, as said below
- master: float32 [512, 1024], P('row', 'col')
- velocity: float32 [512, 1024], P('row', 'col'), may hold values from -0.6 to 0.6
- bn_params: float32 [2, 1024], replicated, may hold values from 0.5 to 1.5
- bn_velocity: float32 [2, 1024], replicated, may hold values from -0.6 to 0.6
Outputs:
- input_grad: bfloat16 [384, 49, 512], P(('row', 'col'))
- new_master: float32 [512, 1024], P('row', 'col')
- new_velocity: float32 [512, 1024], P('row', 'col')
- new_weights: bfloat16 [512, 1024], replicated
- new_bn: float32 [2, 1024], replicated
- new_bn_velocity: float32 [2, 1024], replicated
The draws below stay inside these ranges and needn't reach their ends.
Inputs may be any that keep to these rules, and one draw needn't show every extreme that they name: weights lies within one bfloat16 rounding of master, entry by entry.
All inputs are finite; a program needn't handle non-finite values.
Results may differ from the reference program's by a relative error of at most 0.0045.
The reference program's roundings to bfloat16 on the way count: a program that leaves them out, or rounds other values in their place, can miss the bound.
Values may be sent and summed in bfloat16 or wider, within the bound.
A program may use at most 64 MiB of HBM per device.

```python
import math
import jax
import jax.numpy as jnp
from jax import lax

CIN = 512
COUT = 1024
PIX = 49
IMG_DEV = 12
BATCH = 384
N_ROW = 8
N_COL = 4


def weight_field(key, spread):
    base = jax.random.normal(key, (CIN, COUT), jnp.float32)
    row_frac = jnp.arange(CIN, dtype=jnp.float32) / max(CIN - 1, 1)
    col_frac = jnp.arange(COUT, dtype=jnp.float32) / max(COUT - 1, 1)
    ramp = jnp.exp(math.log(10.0) * spread * (row_frac[:, None] + col_frac[None, :] - 1.0))
    return 2.0 * base * ramp


def draw_master(key, part):
    spread = 0.5
    field = weight_field(key, spread)
    key = jax.random.fold_in(key, 3)
    jitter = jax.random.uniform(key, (CIN, COUT), jnp.float32, -1.0, 1.0)
    return field * (1.0 + 0.000244140625 * jitter)


def draw_weights(key, part):
    spread = 0.5
    field = weight_field(key, spread)
    key = jax.random.fold_in(key, 5)
    jitter = jax.random.uniform(key, (CIN, COUT), jnp.float32, -1.0, 1.0)
    return (field * (1.0 + 0.000244140625 * jitter)).astype(jnp.bfloat16)


def draw_activations(key, part):
    key = jax.random.fold_in(key, 7)
    noise_key, pair_key = jax.random.split(key)
    base = jax.random.normal(noise_key, (BATCH, PIX, CIN), jnp.float32)
    image = jnp.arange(BATCH) // IMG_DEV
    column = image % N_COL
    image_ramp = jnp.exp(math.log(3.0) * column.astype(jnp.float32) / max(N_COL - 1, 1))
    offset = jax.random.randint(pair_key, (), 0, N_ROW)
    block = (image + offset) % N_ROW
    chan_block = jnp.arange(CIN) // (CIN // N_ROW)
    boost = jnp.where(block[:, None] == chan_block[None, :], 3.0, 1.0)
    chan_ramp = jnp.exp(math.log(10.0) * jnp.arange(CIN, dtype=jnp.float32) / max(CIN - 1, 1))
    values = jnp.maximum(base, 0.0) * image_ramp[:, None, None] * (boost * chan_ramp[None, :])[:, None, :]
    return values.astype(jnp.bfloat16)


def steps_of(own_key, shape, cuts, least, largest):
    loudness = 1.0
    for position, blocks in cuts:
        heights = jax.random.uniform(jax.random.fold_in(jax.random.fold_in(own_key, 6), position), (blocks,), jnp.float32, least / len(cuts), largest / len(cuts))
        loudness = loudness * jnp.repeat(jnp.exp(heights), shape[position] // blocks).reshape((-1,) + (1,) * (len(shape) - 1 - position))
    return loudness


def bell_draw(own_key, shape, deviation, most, shards=(), kind=jnp.bfloat16):
    array = jax.random.normal(own_key, shape, jnp.float32) * deviation
    if len(shards) > 0:
        array = steps_of(own_key, shape, shards, -0.22, 0.18) * array
    return jnp.clip(array, min=-most, max=most).astype(kind)


def setup_inputs(seed: int = 0) -> dict:
    seeds = jax.random.split(jax.random.key(seed), 9)
    activations = draw_activations(jax.random.fold_in(seeds[8], 71), 0)
    pre_activation = bell_draw(seeds[1], (BATCH, PIX, COUT), 1.0, 6.0, ((0, 32),))
    pooled_grad = bell_draw(seeds[2], (BATCH, COUT), 50.0, 300.0, ((0, 32),), jnp.float32)
    weights = draw_weights(jax.random.fold_in(seeds[8], 71), 0)
    master = draw_master(jax.random.fold_in(seeds[8], 71), 0)
    velocity = bell_draw(seeds[5], (CIN, COUT), 0.1, 0.6, ((0, 8), (1, 4)), jnp.float32)
    bn_params = jnp.clip(1.0 + 0.1 * jax.random.normal(seeds[6], (2, COUT), jnp.float32), 0.5, 1.5)
    bn_velocity = bell_draw(seeds[7], (2, COUT), 0.1, 0.6, (), jnp.float32)
    return {"activations": activations, "pre_activation": pre_activation, "pooled_grad": pooled_grad, "weights": weights, "master": master, "velocity": velocity, "bn_params": bn_params, "bn_velocity": bn_velocity}


epsilon = 1e-05
trust_coef = 0.001
weight_decay = 0.0001
momentum = 0.9
learn_rate = 12.0

def reference(activations, pre_activation, pooled_grad, weights, master, velocity, bn_params, bn_velocity):
    group_images = N_COL * IMG_DEV
    element_count = group_images * PIX
    norm_scale_weight = bn_params[0]
    acts_grouped = activations.reshape(N_ROW, group_images, PIX, CIN)
    pre_grouped = pre_activation.reshape(N_ROW, group_images, PIX, COUT)
    pooled_grouped = pooled_grad.reshape(N_ROW, group_images, COUT)

    def group_step(carry, pieces):
        acts, preact, pooled = pieces
        flat_in = acts.reshape(element_count, CIN)
        conv_low = jnp.dot(flat_in, weights, preferred_element_type=jnp.float32).astype(jnp.bfloat16)
        expand_conv_output = lax.optimization_barrier(conv_low).astype(jnp.float32)
        group_mean_value = lax.optimization_barrier(jnp.sum(expand_conv_output, axis=0)) / element_count
        variance = lax.optimization_barrier(jnp.sum(expand_conv_output * expand_conv_output, axis=0)) / element_count - group_mean_value * group_mean_value
        inverse_deviation = lax.rsqrt(variance + epsilon)
        upstream_all = jnp.broadcast_to((pooled / PIX)[:, None, :], preact.shape).reshape(element_count, COUT)
        incoming_gradient = jnp.where(preact.reshape(element_count, COUT) > 0, upstream_all, jnp.zeros_like(upstream_all))
        normalized_input = (expand_conv_output - group_mean_value) * inverse_deviation
        upstream_sum_local = lax.optimization_barrier(jnp.sum(incoming_gradient, axis=0))
        upstream_normalized_sum = lax.optimization_barrier(jnp.sum(incoming_gradient * normalized_input, axis=0))
        expand_conv_gradient = (norm_scale_weight * inverse_deviation * (incoming_gradient - upstream_sum_local / element_count - normalized_input * upstream_normalized_sum / element_count)).astype(jnp.bfloat16)
        back = lax.dot_general(expand_conv_gradient, weights, (((1,), (1,)), ((), ())), preferred_element_type=jnp.float32).astype(jnp.bfloat16)
        wgrad = lax.dot_general(flat_in, expand_conv_gradient, (((0,), (0,)), ((), ())), preferred_element_type=jnp.float32)
        return ((carry[0] + wgrad, carry[1] + upstream_normalized_sum, carry[2] + upstream_sum_local), back)
    start = (jnp.zeros((CIN, COUT), jnp.float32), jnp.zeros((COUT,), jnp.float32), jnp.zeros((COUT,), jnp.float32))
    totals, backs = lax.scan(group_step, start, (acts_grouped, pre_grouped, pooled_grouped))
    input_grad = backs.reshape(BATCH, PIX, CIN)
    inv_batch = 1.0 / BATCH
    weight_grad = totals[0] * inv_batch
    bn_grad = jnp.stack([totals[1], totals[2]]) * inv_batch
    wnorm = jnp.sqrt(jnp.sum(master * master))
    gnorm = jnp.sqrt(jnp.sum(weight_grad * weight_grad))
    trust = trust_coef * wnorm / (gnorm + weight_decay * wnorm)
    new_velocity = momentum * velocity + learn_rate * trust * (weight_grad + weight_decay * master)
    new_master = master - new_velocity
    new_weights = new_master.astype(jnp.bfloat16)
    new_bn_velocity = momentum * bn_velocity + learn_rate * bn_grad
    new_bn = bn_params - new_bn_velocity
    return (input_grad, new_master, new_velocity, new_weights, new_bn, new_bn_velocity)
```

```python
import functools

import jax
import jax.numpy as jnp
from jax import lax
from jax.experimental import pallas as pl
from jax.experimental.pallas import tpu as pltpu
from jax.sharding import PartitionSpec as P

epsilon = 1e-05
trust_coef = 0.001
weight_decay = 0.0001
momentum = 0.9
learn_rate = 12.0


def body(
    activations, pre_activation, pooled_grad, weights, master, velocity, bn_params, bn_velocity
):
    images, positions, in_chan = activations.shape
    out_chan = weights.shape[1]
    row_count = images * positions
    n_row = lax.axis_size("row")
    n_col = lax.axis_size("col")
    group_element_count = row_count * n_col
    total_images = images * n_row * n_col
    norm_scale_weight = bn_params[0]
    flat_in = activations.reshape(row_count, in_chan)
    conv_low = jnp.dot(flat_in, weights, preferred_element_type=jnp.float32).astype(jnp.bfloat16)
    expand_conv_output = lax.optimization_barrier(conv_low).astype(jnp.float32)
    stats = lax.psum(
        (
            jnp.sum(expand_conv_output, axis=0),
            jnp.sum(expand_conv_output * expand_conv_output, axis=0),
        ),
        "col",
    )
    group_mean_value = stats[0] / group_element_count
    variance = stats[1] / group_element_count - group_mean_value * group_mean_value
    inverse_deviation = lax.rsqrt(variance + epsilon)
    upstream_all = jnp.broadcast_to(
        (pooled_grad / positions)[:, None, :], pre_activation.shape
    ).reshape(row_count, out_chan)
    incoming_gradient = jnp.where(
        pre_activation.reshape(row_count, out_chan) > 0, upstream_all, jnp.zeros_like(upstream_all)
    )
    normalized_input = (expand_conv_output - group_mean_value) * inverse_deviation
    local_up = jnp.sum(incoming_gradient, axis=0)
    local_upstream_normalized = jnp.sum(incoming_gradient * normalized_input, axis=0)
    group_totals_reduced = lax.psum((local_up, local_upstream_normalized), "col")
    expand_conv_gradient = (
        norm_scale_weight
        * inverse_deviation
        * (
            incoming_gradient
            - group_totals_reduced[0] / group_element_count
            - normalized_input * group_totals_reduced[1] / group_element_count
        )
    ).astype(jnp.bfloat16)
    back = lax.dot_general(
        expand_conv_gradient, weights, (((1,), (1,)), ((), ())), preferred_element_type=jnp.float32
    )
    input_grad = back.astype(jnp.bfloat16).reshape(images, positions, in_chan)
    row_part = lax.psum_scatter(
        lax.dot_general(
            flat_in,
            expand_conv_gradient,
            (((0,), (0,)), ((), ())),
            preferred_element_type=jnp.float32,
        ),
        "row",
        scatter_dimension=0,
        tiled=True,
    )
    grad_sum = lax.psum_scatter(row_part, "col", scatter_dimension=1, tiled=True)
    weight_grad = grad_sum * (1.0 / total_images)
    master_sq = jnp.sum(master * master)
    grad_sq = jnp.sum(weight_grad * weight_grad)
    bn_tot = lax.psum((group_totals_reduced[1], group_totals_reduced[0]), "row")
    norms = lax.psum((master_sq, grad_sq), ("row", "col"))
    upx_total, up_total = (bn_tot[0], bn_tot[1])
    master_total, grad_total = (norms[0], norms[1])
    wnorm = jnp.sqrt(master_total)
    gnorm = jnp.sqrt(grad_total)
    trust = trust_coef * wnorm / (gnorm + weight_decay * wnorm)
    new_velocity = momentum * velocity + learn_rate * trust * (weight_grad + weight_decay * master)
    new_master = master - new_velocity
    shard_low = new_master.astype(jnp.bfloat16)
    wide_rows = lax.all_gather(shard_low, "col", axis=1, tiled=True)
    new_weights = lax.all_gather(wide_rows, "row", axis=0, tiled=True)
    bn_grad = jnp.stack([upx_total, up_total]) * (1.0 / total_images)
    new_bn_velocity = momentum * bn_velocity + learn_rate * bn_grad
    new_bn = bn_params - new_bn_velocity
    return (input_grad, new_master, new_velocity, new_weights, new_bn, new_bn_velocity)


MESH = pl.DeviceIdType.MESH
PAD = 64
CW = 256


def flip(value, bit):
    return lax.rem(value + bit, 2)


def kernel(
    act_hbm, pre_hbm, pool_ref, w_hbm, master_ref, velocity_ref, bn_ref, bnv_ref,
    ig_hbm, nm_ref, nv_ref, nw_hbm, nbn_ref, nbv_ref,
    act, pre, w, a_s, at, conv, cg, poolg, ig, wout,
    st_s, st_r, bn_s, bn_r, sa, ra, own, sb, rb, sc, rc, sd, rd, acc, n1s, n1r, n2s, n2r,
    in_sem, out_sem, st_ss, st_rs, bn_ss, bn_rs, a_ss, a_rs, b_ss, b_rs, c_ss, c_rs, d_ss, d_rs,
    n1_ss, n1_rs, n2_ss, n2_rs, z_ss, z_rs, f_ss, f_rs, g_ss, g_rs, k_ss, k_rs,
):
    images, positions, in_chan = act.shape
    out_chan = w.shape[1]
    n_row, n_col = 8, 4
    rblk, cblk = in_chan // n_row, out_chan // n_col
    half = out_chan // 2
    device_count = images * positions
    count = device_count * n_col
    total_images = images * n_row * n_col
    r, z = lax.axis_index("row"), lax.axis_index("col")
    k, x, y = lax.rem(r, 2), lax.rem(r // 2, 2), r // 4

    def row_of(yy, xx, kk):
        return 4 * yy + 2 * xx + kk

    def row_peer(j):
        return row_of(flip(y, j // 4), flip(x, (j // 2) % 2), flip(k, j % 2))

    def col_peer(i):
        return 2 * flip(z // 2, i // 2) + flip(lax.rem(z, 2), i % 2)

    def send(src, dst, ss, rs, row, col):
        copy = pltpu.make_async_remote_copy(
            src_ref=src, dst_ref=dst, send_sem=ss, recv_sem=rs,
            device_id=(row, col), device_id_type=MESH,
        )
        copy.start()
        return copy

    barrier = pltpu.get_barrier_semaphore()
    for j in range(1, n_row):
        pl.semaphore_signal(barrier, inc=1, device_id=(row_peer(j), z), device_id_type=MESH)
    for i in range(1, n_col):
        pl.semaphore_signal(barrier, inc=1, device_id=(r, col_peer(i)), device_id_type=MESH)

    loads = [
        pltpu.make_async_copy(src, dst, in_sem.at[n])
        for n, (src, dst) in enumerate(((act_hbm, act), (w_hbm, w), (pre_hbm, pre)))
    ]
    for load in loads:
        load.start()

    cg[...] = jnp.zeros_like(cg)
    a_s[...] = jnp.zeros_like(a_s)
    poolg[...] = pool_ref[...] / positions
    st_s[...] = jnp.zeros_like(st_s)
    msq = jnp.sum(master_ref[...] * master_ref[...], axis=0, keepdims=True)
    m_part = functools.reduce(lambda p, q: p + q, [msq[:, c : c + 128] for c in range(0, cblk, 128)])

    loads[0].wait()
    for im in range(images):
        a_s[PAD * im : PAD * im + positions, :] = act[im]
    loads[1].wait()
    loads[2].wait()
    for c in range(0, out_chan, CW):
        cols = slice(c, c + CW)
        low = jnp.dot(a_s[...], w[:, cols], preferred_element_type=jnp.float32).astype(jnp.bfloat16)
        conv[:, cols] = low
        wide = low.astype(jnp.float32)
        total = jnp.sum(wide, axis=0, keepdims=True)
        mean = total / device_count
        st_s[0:1, cols] = total
        st_s[1:2, cols] = jnp.sum(wide * wide, axis=0, keepdims=True)
        up_sum = jnp.zeros((1, CW), jnp.float32)
        upx_sum = jnp.zeros((1, CW), jnp.float32)
        for im in range(images):
            rows = conv[PAD * im : PAD * im + positions, cols].astype(jnp.float32)
            keep = pre[im, :, cols].astype(jnp.float32) > 0
            pooled = poolg[im : im + 1, cols]
            up_sum += pooled * jnp.sum(jnp.where(keep, 1.0, 0.0), axis=0, keepdims=True)
            upx_sum += pooled * jnp.sum(jnp.where(keep, rows - mean, 0.0), axis=0, keepdims=True)
        st_s[2:3, cols] = up_sum
        st_s[3:4, cols] = upx_sum

    pl.semaphore_wait(barrier, n_row + n_col - 2)
    sends = []
    st = [
        send(st_s, st_r.at[i - 1], st_ss.at[i - 1], st_rs.at[i - 1], r, col_peer(i))
        for i in range(1, n_col)
    ]
    turned = a_s[...].T
    for q in range(n_row):
        at[q % 2, (q // 2) * rblk : (q // 2 + 1) * rblk, :] = turned[q * rblk : (q + 1) * rblk, :]
    for copy in st:
        copy.wait_recv()
    parts = [st_s[...]] + [st_r[i] for i in range(n_col - 1)]
    mu = (parts[0][0:1] + parts[1][0:1] + parts[2][0:1] + parts[3][0:1]) / count
    square = parts[0][1:2] + parts[1][1:2] + parts[2][1:2] + parts[3][1:2]
    su = parts[0][2:3] + parts[1][2:3] + parts[2][2:3] + parts[3][2:3]
    rstd = lax.rsqrt(square / count - mu * mu + epsilon)
    sx = jnp.zeros_like(mu)
    for part in parts:
        sx += part[3:4] + (part[0:1] / device_count - mu) * part[2:3]
    sx = sx * rstd
    bn_s[0:1, :] = sx
    bn_s[1:2, :] = su
    bn = [
        send(bn_s, bn_r.at[j - 1], bn_ss.at[j - 1], bn_rs.at[j - 1], row_peer(j), z)
        for j in range(1, n_row)
    ]
    scale = bn_ref[0:1, :] * rstd
    shift = scale * su / count
    slope = scale * rstd * sx / count

    def grad_columns(c):
        cols = slice(c, c + CW)
        for im in range(images):
            span = slice(PAD * im, PAD * im + positions)
            rows = conv[span, cols].astype(jnp.float32)
            keep = pre[im, :, cols].astype(jnp.float32) > 0
            up = jnp.where(keep, scale[:, cols] * poolg[im : im + 1, cols], 0.0)
            grad = up - shift[:, cols] - slope[:, cols] * (rows - mu[:, cols])
            cg[span, cols] = grad.astype(jnp.bfloat16)

    core = []
    for h in range(2):
        for c in range(h * half, (h + 1) * half, CW):
            grad_columns(c)
        block = jnp.dot(at[1 - k], cg[:, h * half : (h + 1) * half], preferred_element_type=jnp.float32)
        sa[h] = block.reshape(4, rblk, half)
        core.append(send(sa.at[h], ra.at[h], a_ss.at[h], a_rs.at[h], row_of(y, x, 1 - k), z))
    for h in range(2):
        block = jnp.dot(at[k], cg[:, h * half : (h + 1) * half], preferred_element_type=jnp.float32)
        own[h] = block.reshape(4, rblk, half)

    x_peer, y_peer = row_of(y, 1 - x, k), row_of(1 - y, x, k)
    first, second = (x_peer, y_peer), (y_peer, x_peer)

    def keep_q(h, j):
        return 2 * j + x if h == 0 else 2 * y + j

    def send_q(h, j):
        return 2 * j + 1 - x if h == 0 else 2 * (1 - y) + j

    step_b = []
    for h in range(2):
        core[h].wait_recv()
        for j in range(2):
            q = send_q(h, j)
            sb[h, j] = (own[h, q] + ra[h, q]).astype(jnp.bfloat16)
        step_b.append(send(sb.at[h], rb.at[h], b_ss.at[h], b_rs.at[h], first[h], z))

    def input_rows(lo, hi):
        back = lax.dot_general(
            cg[PAD * lo : PAD * hi, :], w[...], (((1,), (1,)), ((), ())),
            preferred_element_type=jnp.float32,
        ).astype(jnp.bfloat16)
        for im in range(lo, hi):
            ig[im] = back[PAD * (im - lo) : PAD * (im - lo) + positions, :]

    input_rows(0, images // 2)
    step_c = []
    for h in range(2):
        step_b[h].wait_recv()
        near = 1 - y if h == 0 else 1 - x
        q = keep_q(h, near)
        sc[h] = (own[h, q] + ra[h, q] + rb[h, near].astype(jnp.float32)).astype(jnp.bfloat16)
        step_c.append(send(sc.at[h], rc.at[h], c_ss.at[h], c_rs.at[h], second[h], z))
    input_rows(images // 2, images)
    out_copies = [pltpu.make_async_copy(ig, ig_hbm, out_sem.at[0])]
    out_copies[0].start()
    for h in range(2):
        step_c[h].wait_recv()
        mine = y if h == 0 else x
        q = 2 * y + x
        done = own[h, q] + ra[h, q] + rb[h, mine].astype(jnp.float32) + rc[h].astype(jnp.float32)
        acc[2 * h] = done[:, :cblk]
        acc[2 * h + 1] = done[:, cblk:]
    step_d = []
    for i in range(1, n_col):
        sd[i - 1] = acc[col_peer(i)].astype(jnp.bfloat16)
        step_d.append(send(sd.at[i - 1], rd.at[i - 1], d_ss.at[i - 1], d_rs.at[i - 1], r, col_peer(i)))
    grad = acc[z]
    for i in range(n_col - 1):
        step_d[i].wait_recv()
        grad += rd[i].astype(jnp.float32)
    grad = grad * (1.0 / total_images)

    gsq = jnp.sum(grad * grad, axis=0, keepdims=True)
    g_part = functools.reduce(lambda p, q: p + q, [gsq[:, c : c + 128] for c in range(0, cblk, 128)])
    n1s[...] = jnp.zeros_like(n1s)
    n1s[0:1, :] = g_part
    n1s[1:2, :] = m_part
    norm1 = [
        send(n1s, n1r.at[j - 1], n1_ss.at[j - 1], n1_rs.at[j - 1], row_peer(j), z)
        for j in range(1, n_row)
    ]
    norm = n1s[...]
    for j in range(n_row - 1):
        norm1[j].wait_recv()
        norm += n1r[j]
    n2s[...] = norm
    norm2 = [
        send(n2s, n2r.at[i - 1], n2_ss.at[i - 1], n2_rs.at[i - 1], r, col_peer(i))
        for i in range(1, n_col)
    ]
    for i in range(n_col - 1):
        norm2[i].wait_recv()
        norm += n2r[i]
    gnorm = jnp.sqrt(jnp.sum(norm[0:1, :], axis=1, keepdims=True))
    wnorm = jnp.sqrt(jnp.sum(norm[1:2, :], axis=1, keepdims=True))
    trust = trust_coef * wnorm / (gnorm + weight_decay * wnorm)
    weights_now = master_ref[...]
    new_velocity = momentum * velocity_ref[...] + learn_rate * trust * (grad + weight_decay * weights_now)
    new_master = weights_now - new_velocity
    nv_ref[...] = new_velocity
    nm_ref[...] = new_master

    def block(row, p):
        rows = pl.ds(pl.multiple_of(row * rblk, rblk), rblk)
        return wout.at[rows, pl.ds(pl.multiple_of(p * cblk, cblk), cblk)]

    def order(i):
        return col_peer(i)

    wout[pl.ds(pl.multiple_of(r * rblk, rblk), rblk), pl.ds(pl.multiple_of(z * cblk, cblk), cblk)] = (
        new_master.astype(jnp.bfloat16)
    )
    zs = [
        send(block(r, z), block(r, z), z_ss.at[i - 1], z_rs.at[i - 1], r, col_peer(i))
        for i in range(1, n_col)
    ]
    sibling = row_of(y, x, 1 - k)

    def near_row(p):
        h = p // 2
        return row_of(flip(y, 1 - h), flip(x, h), k)

    def far_row(p):
        h = p // 2
        return row_of(flip(y, h), flip(x, 1 - h), k)

    def to_sibling(row, p, slot):
        sends.append(send(block(row, p), block(row, p), k_ss.at[slot], k_rs.at[slot], sibling, z))

    near_sends, far_sends = [], []
    for i in range(n_col):
        p = order(i)
        if i > 0:
            src = block(r, p)
            pltpu.make_async_remote_copy(
                src_ref=src, dst_ref=src, send_sem=z_ss.at[i - 1], recv_sem=z_rs.at[i - 1],
                device_id=(r, p), device_id_type=MESH,
            ).wait_recv()
        near_sends.append(send(block(r, p), block(r, p), f_ss.at[i], f_rs.at[i], near_row(p), z))
        far_sends.append(send(block(r, p), block(r, p), g_ss.at[i], g_rs.at[i], far_row(p), z))
        to_sibling(r, p, i)

    def arrived(row, p, ss, rs, source):
        ref = block(row, p)
        pltpu.make_async_remote_copy(
            src_ref=ref, dst_ref=ref, send_sem=ss, recv_sem=rs, device_id=(source, z), device_id_type=MESH
        ).wait_recv()

    for i in range(n_col):
        p = order(i)
        got = near_row(p)
        arrived(got, p, f_ss.at[i], f_rs.at[i], got)
        far_sends.append(
            send(block(got, p), block(got, p), g_ss.at[4 + i], g_rs.at[4 + i], far_row(p), z)
        )
        to_sibling(got, p, 4 + i)
    diagonal = row_of(1 - y, 1 - x, k)
    for i in range(n_col):
        p = order(i)
        source = far_row(p)
        arrived(source, p, g_ss.at[i], g_rs.at[i], source)
        to_sibling(source, p, 8 + i)
    for i in range(n_col):
        p = order(i)
        arrived(diagonal, p, g_ss.at[4 + i], g_rs.at[4 + i], far_row(p))
        to_sibling(diagonal, p, 12 + i)

    sums = bn_s[...]
    for j in range(n_row - 1):
        bn[j].wait_recv()
        sums += bn_r[j]
    new_bnv = momentum * bnv_ref[...] + learn_rate * (sums * (1.0 / total_images))
    nbv_ref[...] = new_bnv
    nbn_ref[...] = bn_ref[...] - new_bnv

    for i in range(n_col):
        p = order(i)
        rows = (r, near_row(p), far_row(p), diagonal)
        for n in range(4):
            arrived(rows[n] + 1 - 2 * k, p, k_ss.at[4 * n + i], k_rs.at[4 * n + i], sibling)
    out_copies.append(pltpu.make_async_copy(wout, nw_hbm, out_sem.at[1]))
    out_copies[1].start()
    for copy in st + bn + core + step_b + step_c + step_d + norm1 + norm2 + zs + near_sends + far_sends + sends:
        copy.wait_send()
    for copy in out_copies:
        copy.wait()


def fused(activations, pre_activation, pooled_grad, weights, master, velocity, bn_params, bn_velocity):
    images, positions, in_chan = activations.shape
    out_chan = weights.shape[1]
    rows = images * PAD
    rblk, cblk = master.shape
    half = out_chan // 2
    f32, bf16 = jnp.float32, jnp.bfloat16
    vmem = pl.BlockSpec(memory_space=pltpu.VMEM)
    hbm = pl.BlockSpec(memory_space=pl.ANY)
    dma = pltpu.SemaphoreType.DMA
    pairs = (3, 7, 2, 2, 2, 3, 7, 3, 3, 4, 8, 16)
    flops = 6 * images * positions * in_chan * out_chan
    return pl.pallas_call(
        kernel,
        out_shape=(
            jax.ShapeDtypeStruct(activations.shape, bf16),
            jax.ShapeDtypeStruct(master.shape, f32),
            jax.ShapeDtypeStruct(master.shape, f32),
            jax.ShapeDtypeStruct(weights.shape, bf16),
            jax.ShapeDtypeStruct(bn_params.shape, f32),
            jax.ShapeDtypeStruct(bn_params.shape, f32),
        ),
        in_specs=[hbm, hbm, vmem, hbm, vmem, vmem, vmem, vmem],
        out_specs=(hbm, vmem, vmem, hbm, vmem, vmem),
        scratch_shapes=[
            pltpu.VMEM(activations.shape, bf16),
            pltpu.VMEM(pre_activation.shape, bf16),
            pltpu.VMEM(weights.shape, bf16),
            pltpu.VMEM((rows, in_chan), bf16),
            pltpu.VMEM((2, in_chan // 2, rows), bf16),
            pltpu.VMEM((rows, out_chan), bf16),
            pltpu.VMEM((rows, out_chan), bf16),
            pltpu.VMEM(pooled_grad.shape, f32),
            pltpu.VMEM(activations.shape, bf16),
            pltpu.VMEM(weights.shape, bf16),
            pltpu.VMEM((4, out_chan), f32),
            pltpu.VMEM((3, 4, out_chan), f32),
            pltpu.VMEM((2, out_chan), f32),
            pltpu.VMEM((7, 2, out_chan), f32),
            pltpu.VMEM((2, 4, rblk, half), f32),
            pltpu.VMEM((2, 4, rblk, half), f32),
            pltpu.VMEM((2, 4, rblk, half), f32),
            pltpu.VMEM((2, 2, rblk, half), bf16),
            pltpu.VMEM((2, 2, rblk, half), bf16),
            pltpu.VMEM((2, rblk, half), bf16),
            pltpu.VMEM((2, rblk, half), bf16),
            pltpu.VMEM((3, rblk, cblk), bf16),
            pltpu.VMEM((3, rblk, cblk), bf16),
            pltpu.VMEM((4, rblk, cblk), f32),
            pltpu.VMEM((8, 128), f32),
            pltpu.VMEM((7, 8, 128), f32),
            pltpu.VMEM((8, 128), f32),
            pltpu.VMEM((3, 8, 128), f32),
            dma((3,)),
            dma((2,)),
        ]
        + [dma((n,)) for n in pairs for _ in range(2)],
        compiler_params=pltpu.CompilerParams(
            collective_id=0, has_side_effects=True, vmem_limit_bytes=48 * 1024 * 1024
        ),
        cost_estimate=pl.CostEstimate(flops=flops, bytes_accessed=8 * 1024 * 1024, transcendentals=0),
    )(activations, pre_activation, pooled_grad, weights, master, velocity, bn_params, bn_velocity)


def pick(mesh):
    if mesh.shape["row"] == 8 and mesh.shape["col"] == 4:
        return fused
    return body


def solution(mesh):
    placed = (
        P(("row", "col"), None, None),
        P(("row", "col"), None, None),
        P(("row", "col"), None),
        P(),
        P("row", "col"),
        P("row", "col"),
        P(),
        P(),
    )
    return jax.shard_map(
        pick(mesh),
        mesh=mesh,
        in_specs=placed,
        out_specs=(P(("row", "col"), None, None), P("row", "col"), P("row", "col"), P(), P(), P()),
        check_vma=False,
    )
```

```python
import functools

import jax
import jax.numpy as jnp
from jax import lax
from jax.experimental import pallas as pl
from jax.experimental.pallas import tpu as pltpu
from jax.sharding import PartitionSpec as P

epsilon = 1e-05
trust_coef = 0.001
weight_decay = 0.0001
momentum = 0.9
learn_rate = 12.0


def body(
    activations, pre_activation, pooled_grad, weights, master, velocity, bn_params, bn_velocity
):
    images, positions, in_chan = activations.shape
    out_chan = weights.shape[1]
    row_count = images * positions
    n_row = lax.axis_size("row")
    n_col = lax.axis_size("col")
    group_element_count = row_count * n_col
    total_images = images * n_row * n_col
    norm_scale_weight = bn_params[0]
    flat_in = activations.reshape(row_count, in_chan)
    conv_low = jnp.dot(flat_in, weights, preferred_element_type=jnp.float32).astype(jnp.bfloat16)
    expand_conv_output = lax.optimization_barrier(conv_low).astype(jnp.float32)
    stats = lax.psum(
        (
            jnp.sum(expand_conv_output, axis=0),
            jnp.sum(expand_conv_output * expand_conv_output, axis=0),
        ),
        "col",
    )
    group_mean_value = stats[0] / group_element_count
    variance = stats[1] / group_element_count - group_mean_value * group_mean_value
    inverse_deviation = lax.rsqrt(variance + epsilon)
    upstream_all = jnp.broadcast_to(
        (pooled_grad / positions)[:, None, :], pre_activation.shape
    ).reshape(row_count, out_chan)
    incoming_gradient = jnp.where(
        pre_activation.reshape(row_count, out_chan) > 0, upstream_all, jnp.zeros_like(upstream_all)
    )
    normalized_input = (expand_conv_output - group_mean_value) * inverse_deviation
    local_up = jnp.sum(incoming_gradient, axis=0)
    local_upstream_normalized = jnp.sum(incoming_gradient * normalized_input, axis=0)
    group_totals_reduced = lax.psum((local_up, local_upstream_normalized), "col")
    expand_conv_gradient = (
        norm_scale_weight
        * inverse_deviation
        * (
            incoming_gradient
            - group_totals_reduced[0] / group_element_count
            - normalized_input * group_totals_reduced[1] / group_element_count
        )
    ).astype(jnp.bfloat16)
    back = lax.dot_general(
        expand_conv_gradient, weights, (((1,), (1,)), ((), ())), preferred_element_type=jnp.float32
    )
    input_grad = back.astype(jnp.bfloat16).reshape(images, positions, in_chan)
    row_part = lax.psum_scatter(
        lax.dot_general(
            flat_in,
            expand_conv_gradient,
            (((0,), (0,)), ((), ())),
            preferred_element_type=jnp.float32,
        ),
        "row",
        scatter_dimension=0,
        tiled=True,
    )
    grad_sum = lax.psum_scatter(row_part, "col", scatter_dimension=1, tiled=True)
    weight_grad = grad_sum * (1.0 / total_images)
    master_sq = jnp.sum(master * master)
    grad_sq = jnp.sum(weight_grad * weight_grad)
    bn_tot = lax.psum((group_totals_reduced[1], group_totals_reduced[0]), "row")
    norms = lax.psum((master_sq, grad_sq), ("row", "col"))
    upx_total, up_total = (bn_tot[0], bn_tot[1])
    master_total, grad_total = (norms[0], norms[1])
    wnorm = jnp.sqrt(master_total)
    gnorm = jnp.sqrt(grad_total)
    trust = trust_coef * wnorm / (gnorm + weight_decay * wnorm)
    new_velocity = momentum * velocity + learn_rate * trust * (weight_grad + weight_decay * master)
    new_master = master - new_velocity
    shard_low = new_master.astype(jnp.bfloat16)
    wide_rows = lax.all_gather(shard_low, "col", axis=1, tiled=True)
    new_weights = lax.all_gather(wide_rows, "row", axis=0, tiled=True)
    bn_grad = jnp.stack([upx_total, up_total]) * (1.0 / total_images)
    new_bn_velocity = momentum * bn_velocity + learn_rate * bn_grad
    new_bn = bn_params - new_bn_velocity
    return (input_grad, new_master, new_velocity, new_weights, new_bn, new_bn_velocity)


MESH = pl.DeviceIdType.MESH
PAD = 64
CW = 256


def flip(value, bit):
    return lax.rem(value + bit, 2)


def kernel(
    act_hbm, pre_hbm, pool_hbm, w_hbm, master_hbm, velocity_hbm, bn_hbm, bnv_hbm,
    ig, nm_ref, nv_ref, nw_ref, nbn_ref, nbv_ref,
    act, pre, pool_ref, w, master_ref, velocity_ref, bn_ref, bnv_ref,
    a_s, at, conv, cg, poolg, base, gsum,
    st, bn, sa, ra, own, sb, rb, sc, rc, sd, rd, acc, n1, n2,
    in_sem, st_ss, st_rs, bn_ss, bn_rs, a_ss, a_rs, b_ss, b_rs, c_ss, c_rs, d_ss, d_rs,
    n1_ss, n1_rs, n2_ss, n2_rs, base_ss, base_rs, gsum_ss, gsum_rs,
):
    images, positions, in_chan = act.shape
    out_chan = w.shape[1]
    n_row, n_col = 8, 4
    rblk, cblk = in_chan // n_row, out_chan // n_col
    half = out_chan // 2
    device_count = images * positions
    count = device_count * n_col
    total_images = images * n_row * n_col
    r, z = lax.axis_index("row"), lax.axis_index("col")
    k, x, y = lax.rem(r, 2), lax.rem(r // 2, 2), r // 4

    def row_of(yy, xx, kk):
        return 4 * yy + 2 * xx + kk

    def row_peer(j):
        return row_of(flip(y, j // 4), flip(x, (j // 2) % 2), flip(k, j % 2))

    def col_peer(i):
        return 2 * flip(z // 2, i // 2) + flip(lax.rem(z, 2), i % 2)

    def send(src, dst, ss, rs, row, col):
        copy = pltpu.make_async_remote_copy(
            src_ref=src, dst_ref=dst, send_sem=ss, recv_sem=rs,
            device_id=(row, col), device_id_type=MESH,
        )
        copy.start()
        return copy

    barrier = pltpu.get_barrier_semaphore()
    for j in range(1, n_row):
        pl.semaphore_signal(barrier, inc=1, device_id=(row_peer(j), z), device_id_type=MESH)
    for i in range(1, n_col):
        pl.semaphore_signal(barrier, inc=1, device_id=(r, col_peer(i)), device_id_type=MESH)

    loads = [
        pltpu.make_async_copy(src, dst, in_sem.at[n])
        for n, (src, dst) in enumerate(
            (
                (master_hbm, master_ref),
                (velocity_hbm, velocity_ref),
                (w_hbm, w),
                (act_hbm, act),
                (pool_hbm, pool_ref),
                (pre_hbm, pre),
                (bn_hbm, bn_ref),
                (bnv_hbm, bnv_ref),
            )
        )
    ]
    for load in loads:
        load.start()

    sends = []

    def block(row, p):
        rows = pl.ds(pl.multiple_of(row * rblk, rblk), rblk)
        return rows, pl.ds(pl.multiple_of(p * cblk, cblk), cblk)

    def near_row(p):
        h = p // 2
        return row_of(flip(y, 1 - h), flip(x, h), k)

    def far_row(p):
        h = p // 2
        return row_of(flip(y, h), flip(x, 1 - h), k)

    diagonal = row_of(1 - y, 1 - x, k)
    sibling = row_of(y, x, 1 - k)

    class Gather:
        def __init__(self, buf, ss, rs):
            self.buf, self.ss, self.rs = buf, ss, rs

        def copy(self, row, p, slot, to_row, to_col):
            ref = self.buf.at[block(row, p)]
            return pltpu.make_async_remote_copy(
                src_ref=ref, dst_ref=ref, send_sem=self.ss.at[slot], recv_sem=self.rs.at[slot],
                device_id=(to_row, to_col), device_id_type=MESH,
            )

        def send(self, row, p, slot, to_row, to_col):
            copy = self.copy(row, p, slot, to_row, to_col)
            copy.start()
            sends.append(copy)

        def along_col(self):
            for i in range(1, n_col):
                self.send(r, z, i, r, col_peer(i))

        def own_out(self):
            for i in range(n_col):
                p = col_peer(i)
                if i > 0:
                    self.copy(r, p, i, r, p).wait_recv()
                self.send(r, p, 4 + i, near_row(p), z)
                self.send(r, p, 8 + i, far_row(p), z)
                self.send(r, p, 16 + i, sibling, z)

        def near_out(self):
            for i in range(n_col):
                p = col_peer(i)
                got = near_row(p)
                self.copy(got, p, 4 + i, got, z).wait_recv()
                self.send(got, p, 12 + i, far_row(p), z)
                self.send(got, p, 20 + i, sibling, z)

        def far_out(self):
            for i in range(n_col):
                p = col_peer(i)
                got = far_row(p)
                self.copy(got, p, 8 + i, got, z).wait_recv()
                self.send(got, p, 24 + i, sibling, z)
            for i in range(n_col):
                p = col_peer(i)
                self.copy(diagonal, p, 12 + i, far_row(p), z).wait_recv()
                self.send(diagonal, p, 28 + i, sibling, z)

        def rows(self, p):
            return (r, near_row(p), far_row(p), diagonal)

        def from_sibling(self, n, i):
            p = col_peer(i)
            row = self.rows(p)[n] + 1 - 2 * k
            self.copy(row, p, 16 + 4 * n + i, sibling, z).wait_recv()
            return row, p

    gather_base = Gather(base, base_ss, base_rs)
    gather_grad = Gather(gsum, gsum_ss, gsum_rs)

    cg[...] = jnp.zeros_like(cg)
    a_s[...] = jnp.zeros_like(a_s)
    loads[0].wait()
    loads[1].wait()
    loads[2].wait()
    weights_now = master_ref[...]
    base[block(r, z)] = (
        weights_now - w[block(r, z)].astype(jnp.float32) - momentum * velocity_ref[...]
    ).astype(jnp.bfloat16)
    msq = jnp.sum(weights_now * weights_now, axis=0, keepdims=True)
    m_part = functools.reduce(lambda p, q: p + q, [msq[:, c : c + 128] for c in range(0, cblk, 128)])
    pl.semaphore_wait(barrier, n_row + n_col - 2)
    gather_base.along_col()

    loads[3].wait()
    for im in range(images):
        a_s[PAD * im : PAD * im + positions, :] = act[im]
    loads[4].wait()
    poolg[...] = pool_ref[...] / positions
    loads[5].wait()
    own_st = st.at[z]
    for c in range(0, out_chan, CW):
        cols = slice(c, c + CW)
        low = jnp.dot(a_s[...], w[:, cols], preferred_element_type=jnp.float32).astype(jnp.bfloat16)
        conv[:, cols] = low
        wide = low.astype(jnp.float32)
        total = jnp.sum(wide, axis=0, keepdims=True)
        mean = total / device_count
        own_st[0:1, cols] = total
        own_st[1:2, cols] = jnp.sum(wide * wide, axis=0, keepdims=True)
        up_sum = jnp.zeros((1, CW), jnp.float32)
        upx_sum = jnp.zeros((1, CW), jnp.float32)
        for im in range(images):
            rows = conv[PAD * im : PAD * im + positions, cols].astype(jnp.float32)
            keep = pre[im, :, cols].astype(jnp.float32) > 0
            pooled = poolg[im : im + 1, cols]
            up_sum += pooled * jnp.sum(jnp.where(keep, 1.0, 0.0), axis=0, keepdims=True)
            upx_sum += pooled * jnp.sum(jnp.where(keep, rows - mean, 0.0), axis=0, keepdims=True)
        own_st[2:3, cols] = up_sum
        own_st[3:4, cols] = upx_sum

    stats = [
        send(st.at[z], st.at[z], st_ss.at[i - 1], st_rs.at[i - 1], r, col_peer(i)) for i in range(1, n_col)
    ]
    gather_base.own_out()
    turned = a_s[...].T
    for q in range(n_row):
        at[q % 2, (q // 2) * rblk : (q // 2 + 1) * rblk, :] = turned[q * rblk : (q + 1) * rblk, :]
    for copy in stats:
        copy.wait_recv()
    parts = [st[i] for i in range(n_col)]
    mu = (parts[0][0:1] + parts[1][0:1] + parts[2][0:1] + parts[3][0:1]) / count
    square = parts[0][1:2] + parts[1][1:2] + parts[2][1:2] + parts[3][1:2]
    su = parts[0][2:3] + parts[1][2:3] + parts[2][2:3] + parts[3][2:3]
    rstd = lax.rsqrt(square / count - mu * mu + epsilon)
    sx = jnp.zeros_like(mu)
    for part in parts:
        sx += part[3:4] + (part[0:1] / device_count - mu) * part[2:3]
    sx = sx * rstd
    own_bn = bn.at[r]
    own_bn[0:1, :] = sx
    own_bn[1:2, :] = su
    bns = [
        send(bn.at[r], bn.at[r], bn_ss.at[j - 1], bn_rs.at[j - 1], row_peer(j), z) for j in range(1, n_row)
    ]
    gather_base.near_out()
    loads[6].wait()
    loads[7].wait()
    scale = bn_ref[0:1, :] * rstd
    shift = scale * su / count
    slope = scale * rstd * sx / count

    def grad_columns(c):
        cols = slice(c, c + CW)
        for im in range(images):
            span = slice(PAD * im, PAD * im + positions)
            rows = conv[span, cols].astype(jnp.float32)
            keep = pre[im, :, cols].astype(jnp.float32) > 0
            up = jnp.where(keep, scale[:, cols] * poolg[im : im + 1, cols], 0.0)
            grad = up - shift[:, cols] - slope[:, cols] * (rows - mu[:, cols])
            cg[span, cols] = grad.astype(jnp.bfloat16)

    core = []
    for h in range(2):
        for c in range(h * half, (h + 1) * half, CW):
            grad_columns(c)
        product = jnp.dot(at[1 - k], cg[:, h * half : (h + 1) * half], preferred_element_type=jnp.float32)
        sa[h] = product.reshape(4, rblk, half)
        core.append(send(sa.at[h], ra.at[h], a_ss.at[h], a_rs.at[h], row_of(y, x, 1 - k), z))
    for h in range(2):
        product = jnp.dot(at[k], cg[:, h * half : (h + 1) * half], preferred_element_type=jnp.float32)
        own[h] = product.reshape(4, rblk, half)

    gather_base.far_out()
    x_peer, y_peer = row_of(y, 1 - x, k), row_of(1 - y, x, k)
    first, second = (x_peer, y_peer), (y_peer, x_peer)

    def keep_q(h, j):
        return 2 * j + x if h == 0 else 2 * y + j

    def send_q(h, j):
        return 2 * j + 1 - x if h == 0 else 2 * (1 - y) + j

    step_b = []
    for h in range(2):
        core[h].wait_recv()
        for j in range(2):
            q = send_q(h, j)
            sb[h, j] = (own[h, q] + ra[h, q]).astype(jnp.bfloat16)
        step_b.append(send(sb.at[h], rb.at[h], b_ss.at[h], b_rs.at[h], first[h], z))

    def input_rows(lo, hi):
        back = lax.dot_general(
            cg[PAD * lo : PAD * hi, :], w[...], (((1,), (1,)), ((), ())),
            preferred_element_type=jnp.float32,
        ).astype(jnp.bfloat16)
        for im in range(lo, hi):
            ig[im] = back[PAD * (im - lo) : PAD * (im - lo) + positions, :]

    input_rows(0, images // 2)
    step_c = []
    for h in range(2):
        step_b[h].wait_recv()
        near = 1 - y if h == 0 else 1 - x
        q = keep_q(h, near)
        sc[h] = (own[h, q] + ra[h, q] + rb[h, near].astype(jnp.float32)).astype(jnp.bfloat16)
        step_c.append(send(sc.at[h], rc.at[h], c_ss.at[h], c_rs.at[h], second[h], z))
    input_rows(images // 2, images)
    for h in range(2):
        step_c[h].wait_recv()
        mine = y if h == 0 else x
        q = 2 * y + x
        done = own[h, q] + ra[h, q] + rb[h, mine].astype(jnp.float32) + rc[h].astype(jnp.float32)
        acc[2 * h] = done[:, :cblk]
        acc[2 * h + 1] = done[:, cblk:]
    step_d = []
    for i in range(1, n_col):
        sd[i - 1] = acc[col_peer(i)].astype(jnp.bfloat16)
        step_d.append(send(sd.at[i - 1], rd.at[i - 1], d_ss.at[i - 1], d_rs.at[i - 1], r, col_peer(i)))
    grad = acc[z]
    for i in range(n_col - 1):
        step_d[i].wait_recv()
        grad += rd[i].astype(jnp.float32)
    grad = grad * (1.0 / total_images)

    gsq = jnp.sum(grad * grad, axis=0, keepdims=True)
    g_part = functools.reduce(lambda p, q: p + q, [gsq[:, c : c + 128] for c in range(0, cblk, 128)])
    own_n1 = n1.at[r]
    own_n1[0:1, :] = g_part
    own_n1[1:2, :] = m_part
    norm1 = [
        send(n1.at[r], n1.at[r], n1_ss.at[j - 1], n1_rs.at[j - 1], row_peer(j), z) for j in range(1, n_row)
    ]
    gsum[block(r, z)] = grad.astype(jnp.bfloat16)
    gather_grad.along_col()
    for copy in norm1:
        copy.wait_recv()
    n2[z] = functools.reduce(lambda p, q: p + q, [n1[j] for j in range(n_row)])
    norm2 = [
        send(n2.at[z], n2.at[z], n2_ss.at[i - 1], n2_rs.at[i - 1], r, col_peer(i)) for i in range(1, n_col)
    ]
    gather_grad.own_out()
    for copy in norm2:
        copy.wait_recv()
    norm = functools.reduce(lambda p, q: p + q, [n2[i] for i in range(n_col)])
    gnorm = jnp.sqrt(jnp.sum(norm[0:1, :], axis=1, keepdims=True))
    wnorm = jnp.sqrt(jnp.sum(norm[1:2, :], axis=1, keepdims=True))
    trust = trust_coef * wnorm / (gnorm + weight_decay * wnorm)
    rate = learn_rate * trust
    gather_grad.near_out()
    weights_now = master_ref[...]
    new_velocity = momentum * velocity_ref[...] + rate * (grad + weight_decay * weights_now)
    nv_ref[...] = new_velocity
    nm_ref[...] = weights_now - new_velocity
    for copy in bns:
        copy.wait_recv()
    sums = functools.reduce(lambda p, q: p + q, [bn[j] for j in range(n_row)])
    new_bnv = momentum * bnv_ref[...] + learn_rate * (sums * (1.0 / total_images))
    nbv_ref[...] = new_bnv
    nbn_ref[...] = bn_ref[...] - new_bnv
    gather_grad.far_out()

    def update(row, p):
        at_block = block(row, p)
        low = w[at_block].astype(jnp.float32)
        change = base[at_block].astype(jnp.float32)
        step = rate * (gsum[at_block].astype(jnp.float32) + weight_decay * low)
        nw_ref[at_block] = (low + (change - step)).astype(jnp.bfloat16)

    for n in range(4):
        for i in range(n_col):
            gather_base.from_sibling(n, i)
    for i in range(n_col):
        for row in gather_grad.rows(col_peer(i)):
            update(row, col_peer(i))
    for n in range(4):
        for i in range(n_col):
            update(*gather_grad.from_sibling(n, i))
    for copy in stats + bns + core + step_b + step_c + step_d + norm1 + norm2 + sends:
        copy.wait_send()


def write_out(*refs):
    half = len(refs) // 2
    copies = [
        pltpu.make_async_copy(refs[n], refs[half + n], refs[-1].at[n]) for n in range(half)
    ]
    for copy in copies:
        copy.start()
    for copy in copies:
        copy.wait()


def fused(activations, pre_activation, pooled_grad, weights, master, velocity, bn_params, bn_velocity):
    images, positions, in_chan = activations.shape
    out_chan = weights.shape[1]
    rows = images * PAD
    rblk, cblk = master.shape
    half = out_chan // 2
    f32, bf16 = jnp.float32, jnp.bfloat16
    vmem = pl.BlockSpec(memory_space=pltpu.VMEM)
    hbm = pl.BlockSpec(memory_space=pltpu.HBM)
    dma = pltpu.SemaphoreType.DMA
    pairs = (3, 7, 2, 2, 2, 3, 7, 3, 32, 32)
    flops = 6 * images * positions * in_chan * out_chan
    args = (activations, pre_activation, pooled_grad, weights, master, velocity, bn_params, bn_velocity)
    shapes = tuple(
        jax.ShapeDtypeStruct(a.shape, a.dtype)
        for a in (activations, master, master, weights, bn_params, bn_params)
    )
    results = pl.pallas_call(
        kernel,
        out_shape=shapes,
        in_specs=[hbm] * len(args),
        out_specs=(vmem,) * len(shapes),
        scratch_shapes=[pltpu.VMEM(a.shape, a.dtype) for a in args]
        + [
            pltpu.VMEM((rows, in_chan), bf16),
            pltpu.VMEM((2, in_chan // 2, rows), bf16),
            pltpu.VMEM((rows, out_chan), bf16),
            pltpu.VMEM((rows, out_chan), bf16),
            pltpu.VMEM(pooled_grad.shape, f32),
            pltpu.VMEM(weights.shape, bf16),
            pltpu.VMEM(weights.shape, bf16),
            pltpu.VMEM((4, 4, out_chan), f32),
            pltpu.VMEM((8, 2, out_chan), f32),
            pltpu.VMEM((2, 4, rblk, half), f32),
            pltpu.VMEM((2, 4, rblk, half), f32),
            pltpu.VMEM((2, 4, rblk, half), f32),
            pltpu.VMEM((2, 2, rblk, half), bf16),
            pltpu.VMEM((2, 2, rblk, half), bf16),
            pltpu.VMEM((2, rblk, half), bf16),
            pltpu.VMEM((2, rblk, half), bf16),
            pltpu.VMEM((3, rblk, cblk), bf16),
            pltpu.VMEM((3, rblk, cblk), bf16),
            pltpu.VMEM((4, rblk, cblk), f32),
            pltpu.VMEM((8, 2, 128), f32),
            pltpu.VMEM((4, 2, 128), f32),
            dma((8,)),
        ]
        + [dma((n,)) for n in pairs for _ in range(2)],
        compiler_params=pltpu.CompilerParams(
            collective_id=0, has_side_effects=True, vmem_limit_bytes=32 * 1024 * 1024
        ),
        cost_estimate=pl.CostEstimate(flops=flops, bytes_accessed=8 * 1024 * 1024, transcendentals=0),
    )(*args)
    return pl.pallas_call(
        write_out,
        out_shape=shapes,
        in_specs=[pl.BlockSpec(memory_space=pl.ANY)] * len(shapes),
        out_specs=(hbm,) * len(shapes),
        scratch_shapes=[dma((len(shapes),))],
    )(*results)


def pick(mesh):
    if mesh.shape["row"] == 8 and mesh.shape["col"] == 4:
        return fused
    return body


def solution(mesh):
    placed = (
        P(("row", "col"), None, None),
        P(("row", "col"), None, None),
        P(("row", "col"), None),
        P(),
        P("row", "col"),
        P("row", "col"),
        P(),
        P(),
    )
    return jax.shard_map(
        pick(mesh),
        mesh=mesh,
        in_specs=placed,
        out_specs=(P(("row", "col"), None, None), P("row", "col"), P("row", "col"), P(), P(), P()),
        check_vma=False,
    )
```

```python
import functools

import jax
import jax.numpy as jnp
from jax import lax
from jax.experimental import pallas as pl
from jax.experimental.pallas import tpu as pltpu
from jax.sharding import PartitionSpec as P

epsilon = 1e-05
trust_coef = 0.001
weight_decay = 0.0001
momentum = 0.9
learn_rate = 12.0


def body(
    activations, pre_activation, pooled_grad, weights, master, velocity, bn_params, bn_velocity
):
    images, positions, in_chan = activations.shape
    out_chan = weights.shape[1]
    row_count = images * positions
    n_row = lax.axis_size("row")
    n_col = lax.axis_size("col")
    group_element_count = row_count * n_col
    total_images = images * n_row * n_col
    norm_scale_weight = bn_params[0]
    flat_in = activations.reshape(row_count, in_chan)
    conv_low = jnp.dot(flat_in, weights, preferred_element_type=jnp.float32).astype(jnp.bfloat16)
    expand_conv_output = lax.optimization_barrier(conv_low).astype(jnp.float32)
    stats = lax.psum(
        (
            jnp.sum(expand_conv_output, axis=0),
            jnp.sum(expand_conv_output * expand_conv_output, axis=0),
        ),
        "col",
    )
    group_mean_value = stats[0] / group_element_count
    variance = stats[1] / group_element_count - group_mean_value * group_mean_value
    inverse_deviation = lax.rsqrt(variance + epsilon)
    upstream_all = jnp.broadcast_to(
        (pooled_grad / positions)[:, None, :], pre_activation.shape
    ).reshape(row_count, out_chan)
    incoming_gradient = jnp.where(
        pre_activation.reshape(row_count, out_chan) > 0, upstream_all, jnp.zeros_like(upstream_all)
    )
    normalized_input = (expand_conv_output - group_mean_value) * inverse_deviation
    local_up = jnp.sum(incoming_gradient, axis=0)
    local_upstream_normalized = jnp.sum(incoming_gradient * normalized_input, axis=0)
    group_totals_reduced = lax.psum((local_up, local_upstream_normalized), "col")
    expand_conv_gradient = (
        norm_scale_weight
        * inverse_deviation
        * (
            incoming_gradient
            - group_totals_reduced[0] / group_element_count
            - normalized_input * group_totals_reduced[1] / group_element_count
        )
    ).astype(jnp.bfloat16)
    back = lax.dot_general(
        expand_conv_gradient, weights, (((1,), (1,)), ((), ())), preferred_element_type=jnp.float32
    )
    input_grad = back.astype(jnp.bfloat16).reshape(images, positions, in_chan)
    row_part = lax.psum_scatter(
        lax.dot_general(
            flat_in,
            expand_conv_gradient,
            (((0,), (0,)), ((), ())),
            preferred_element_type=jnp.float32,
        ),
        "row",
        scatter_dimension=0,
        tiled=True,
    )
    grad_sum = lax.psum_scatter(row_part, "col", scatter_dimension=1, tiled=True)
    weight_grad = grad_sum * (1.0 / total_images)
    master_sq = jnp.sum(master * master)
    grad_sq = jnp.sum(weight_grad * weight_grad)
    bn_tot = lax.psum((group_totals_reduced[1], group_totals_reduced[0]), "row")
    norms = lax.psum((master_sq, grad_sq), ("row", "col"))
    upx_total, up_total = (bn_tot[0], bn_tot[1])
    master_total, grad_total = (norms[0], norms[1])
    wnorm = jnp.sqrt(master_total)
    gnorm = jnp.sqrt(grad_total)
    trust = trust_coef * wnorm / (gnorm + weight_decay * wnorm)
    new_velocity = momentum * velocity + learn_rate * trust * (weight_grad + weight_decay * master)
    new_master = master - new_velocity
    shard_low = new_master.astype(jnp.bfloat16)
    wide_rows = lax.all_gather(shard_low, "col", axis=1, tiled=True)
    new_weights = lax.all_gather(wide_rows, "row", axis=0, tiled=True)
    bn_grad = jnp.stack([upx_total, up_total]) * (1.0 / total_images)
    new_bn_velocity = momentum * bn_velocity + learn_rate * bn_grad
    new_bn = bn_params - new_bn_velocity
    return (input_grad, new_master, new_velocity, new_weights, new_bn, new_bn_velocity)


MESH = pl.DeviceIdType.MESH
PAD = 64
LIMIT = 58 * 1024 * 1024


def flip(value, bit):
    return lax.rem(value + bit, 2)


def kernel(
    act_hbm, pre_hbm, pool_hbm, w_hbm, master_hbm, velocity_hbm, bn_hbm, bnv_hbm,
    ig_hbm, nm_hbm, nv_hbm, nw_hbm, nbn_hbm, nbv_hbm,
    act, pre, pool_ref, w, master_ref, velocity_ref, bn_ref, bnv_ref,
    ig, nm_ref, nv_ref, nw_ref, nbn_ref, nbv_ref,
    a_s, at, conv, cg, poolg, base, gsum,
    st, bn, coef, sa, ra, own, sb, rb, sc, rc, sd, rd, n1, n2,
    in_sem, out_sem, st_ss, st_rs, bn_ss, bn_rs, a_ss, a_rs, b_ss, b_rs, c_ss, c_rs, d_ss, d_rs,
    n1_ss, n1_rs, n2_ss, n2_rs, base_ss, base_rs, gsum_ss, gsum_rs,
):
    images, positions, in_chan = act.shape
    out_chan = w.shape[1]
    n_row, n_col = 8, 4
    rblk, cblk = in_chan // n_row, out_chan // n_col
    device_count = images * positions
    count = device_count * n_col
    total_images = images * n_row * n_col
    r, z = lax.axis_index("row"), lax.axis_index("col")
    k, x, y = lax.rem(r, 2), lax.rem(r // 2, 2), r // 4

    def row_of(yy, xx, kk):
        return 4 * yy + 2 * xx + kk

    def row_peer(j):
        return row_of(flip(y, j // 4), flip(x, (j // 2) % 2), flip(k, j % 2))

    def col_peer(i):
        return 2 * flip(z // 2, i // 2) + flip(lax.rem(z, 2), i % 2)

    def send(src, dst, ss, rs, row, col):
        copy = pltpu.make_async_remote_copy(
            src_ref=src, dst_ref=dst, send_sem=ss, recv_sem=rs,
            device_id=(row, col), device_id_type=MESH,
        )
        copy.start()
        return copy

    barrier = pltpu.get_barrier_semaphore()
    for j in range(1, n_row):
        pl.semaphore_signal(barrier, inc=1, device_id=(row_peer(j), z), device_id_type=MESH)
    for i in range(1, n_col):
        pl.semaphore_signal(barrier, inc=1, device_id=(r, col_peer(i)), device_id_type=MESH)

    loads = [
        pltpu.make_async_copy(src, dst, in_sem.at[n])
        for n, (src, dst) in enumerate(
            (
                (master_hbm, master_ref),
                (velocity_hbm, velocity_ref),
                (w_hbm, w),
                (act_hbm, act),
                (pool_hbm, pool_ref),
                (pre_hbm, pre),
                (bn_hbm, bn_ref),
                (bnv_hbm, bnv_ref),
            )
        )
    ]
    for load in loads:
        load.start()

    sends, writes = [], []

    def put(src, dst):
        copy = pltpu.make_async_copy(src, dst, out_sem.at[len(writes)])
        copy.start()
        writes.append(copy)

    def block(row, p):
        rows = pl.ds(pl.multiple_of(row * rblk, rblk), rblk)
        return rows, pl.ds(pl.multiple_of(p * cblk, cblk), cblk)

    def near_row(p):
        h = p // 2
        return row_of(flip(y, 1 - h), flip(x, h), k)

    def far_row(p):
        h = p // 2
        return row_of(flip(y, h), flip(x, 1 - h), k)

    diagonal = row_of(1 - y, 1 - x, k)
    sibling = row_of(y, x, 1 - k)

    class Gather:
        def __init__(self, buf, ss, rs):
            self.buf, self.ss, self.rs = buf, ss, rs

        def copy(self, row, p, slot, to_row, to_col):
            ref = self.buf.at[block(row, p)]
            return pltpu.make_async_remote_copy(
                src_ref=ref, dst_ref=ref, send_sem=self.ss.at[slot], recv_sem=self.rs.at[slot],
                device_id=(to_row, to_col), device_id_type=MESH,
            )

        def send(self, row, p, slot, to_row, to_col):
            copy = self.copy(row, p, slot, to_row, to_col)
            copy.start()
            sends.append(copy)

        def along_col(self):
            for i in range(1, n_col):
                self.send(r, z, i, r, col_peer(i))

        def own_out(self):
            for i in range(n_col):
                p = col_peer(i)
                if i > 0:
                    self.copy(r, p, i, r, p).wait_recv()
                self.send(r, p, 4 + i, near_row(p), z)
                self.send(r, p, 8 + i, far_row(p), z)
                self.send(r, p, 16 + i, sibling, z)

        def near_out(self):
            for i in range(n_col):
                p = col_peer(i)
                got = near_row(p)
                self.copy(got, p, 4 + i, got, z).wait_recv()
                self.send(got, p, 12 + i, far_row(p), z)
                self.send(got, p, 20 + i, sibling, z)

        def far_out(self):
            for i in range(n_col):
                p = col_peer(i)
                got = far_row(p)
                self.copy(got, p, 8 + i, got, z).wait_recv()
                self.send(got, p, 24 + i, sibling, z)
            for i in range(n_col):
                p = col_peer(i)
                self.copy(diagonal, p, 12 + i, far_row(p), z).wait_recv()
                self.send(diagonal, p, 28 + i, sibling, z)

        def rows(self, p):
            return (r, near_row(p), far_row(p), diagonal)

        def from_sibling(self, n, i):
            p = col_peer(i)
            row = self.rows(p)[n] + 1 - 2 * k
            self.copy(row, p, 16 + 4 * n + i, sibling, z).wait_recv()
            return row, p

    gather_base = Gather(base, base_ss, base_rs)
    gather_grad = Gather(gsum, gsum_ss, gsum_rs)

    cg[...] = jnp.zeros_like(cg)
    a_s[...] = jnp.zeros_like(a_s)
    loads[0].wait()
    loads[1].wait()
    loads[2].wait()
    weights_now = master_ref[...]
    base[block(r, z)] = (
        weights_now - w[block(r, z)].astype(jnp.float32) - momentum * velocity_ref[...]
    ).astype(jnp.bfloat16)
    msq = jnp.sum(weights_now * weights_now, axis=0, keepdims=True)
    m_part = functools.reduce(lambda p, q: p + q, [msq[:, c : c + 128] for c in range(0, cblk, 128)])
    loads[3].wait()
    for im in range(images):
        a_s[PAD * im : PAD * im + positions, :] = act[im]
    loads[4].wait()
    poolg[...] = pool_ref[...] / positions
    loads[5].wait()
    stats = []
    for part in range(n_col):
        cols = slice(part * cblk, (part + 1) * cblk)
        own_st = st.at[z, part]
        low = jnp.dot(a_s[...], w[:, cols], preferred_element_type=jnp.float32).astype(jnp.bfloat16)
        conv[:, cols] = low
        wide = low.astype(jnp.float32)
        total = jnp.sum(wide, axis=0, keepdims=True)
        mean = total / device_count
        own_st[0:1, :] = total
        own_st[1:2, :] = jnp.sum(wide * wide, axis=0, keepdims=True)
        up_sum = jnp.zeros((1, cblk), jnp.float32)
        upx_sum = jnp.zeros((1, cblk), jnp.float32)
        for im in range(images):
            rows = conv[PAD * im : PAD * im + positions, cols].astype(jnp.float32)
            keep = pre[im, :, cols].astype(jnp.float32) > 0
            pooled = poolg[im : im + 1, cols]
            up_sum += pooled * jnp.sum(jnp.where(keep, 1.0, 0.0), axis=0, keepdims=True)
            upx_sum += pooled * jnp.sum(jnp.where(keep, rows - mean, 0.0), axis=0, keepdims=True)
        own_st[2:3, :] = up_sum
        own_st[3:4, :] = upx_sum

        if part == 0:
            pl.semaphore_wait(barrier, n_row + n_col - 2)
            gather_base.along_col()
        for i in range(1, n_col):
            slot = n_col * (i - 1) + part
            stats.append(
                send(st.at[z, part], st.at[z, part], st_ss.at[slot], st_rs.at[slot], r, col_peer(i))
            )
    gather_base.own_out()
    turned = a_s[...].T
    for q in range(n_row):
        at[q % 2, (q // 2) * rblk : (q // 2 + 1) * rblk, :] = turned[q * rblk : (q + 1) * rblk, :]
    for copy in stats:
        copy.wait_recv()
    parts = [jnp.concatenate([st[i, part] for part in range(n_col)], axis=1) for i in range(n_col)]
    mu = (parts[0][0:1] + parts[1][0:1] + parts[2][0:1] + parts[3][0:1]) / count
    square = parts[0][1:2] + parts[1][1:2] + parts[2][1:2] + parts[3][1:2]
    su = parts[0][2:3] + parts[1][2:3] + parts[2][2:3] + parts[3][2:3]
    rstd = lax.rsqrt(square / count - mu * mu + epsilon)
    sx = jnp.zeros_like(mu)
    for part in parts:
        sx += part[3:4] + (part[0:1] / device_count - mu) * part[2:3]
    sx = sx * rstd
    own_bn = bn.at[r]
    own_bn[0:1, :] = sx
    own_bn[1:2, :] = su
    bns = [
        send(bn.at[r], bn.at[r], bn_ss.at[j - 1], bn_rs.at[j - 1], row_peer(j), z) for j in range(1, n_row)
    ]
    gather_base.near_out()
    loads[6].wait()
    loads[7].wait()
    scale = bn_ref[0:1, :] * rstd
    coef[0:1, :] = scale
    coef[1:2, :] = scale * su / count
    coef[2:3, :] = scale * rstd * sx / count
    coef[3:4, :] = mu

    order = (3, 1, 2, 0)
    core, step_b, step_c, step_d = [], [], [], []
    corner = 2 * y + x

    def quarter(s):
        p = col_peer(order[s])
        return p, p // 2

    def stage_a(s):
        p, _ = quarter(s)
        cols = pl.ds(pl.multiple_of(p * cblk, cblk), cblk)
        scale_c, shift_c, slope_c, mu_c = (coef[n : n + 1, cols] for n in range(4))
        for im in range(images):
            span = slice(PAD * im, PAD * im + positions)
            rows = conv[span, cols].astype(jnp.float32)
            keep = pre[im, :, cols].astype(jnp.float32) > 0
            up = jnp.where(keep, scale_c * poolg[im : im + 1, cols], 0.0)
            cg[span, cols] = (up - shift_c - slope_c * (rows - mu_c)).astype(jnp.bfloat16)
        product = jnp.dot(at[1 - k], cg[:, cols], preferred_element_type=jnp.float32)
        sa[s] = product.reshape(4, rblk, cblk)
        core.append(send(sa.at[s], ra.at[s], a_ss.at[s], a_rs.at[s], sibling, z))
        product = jnp.dot(at[k], cg[:, cols], preferred_element_type=jnp.float32)
        own[s] = product.reshape(4, rblk, cblk)

    def stage_b(s):
        p, h = quarter(s)
        core[s].wait_recv()
        for j in range(2):
            q = (1 - h) * (2 * j + 1 - x) + h * (2 * (1 - y) + j)
            sb[s, j] = (own[s, q] + ra[s, q]).astype(jnp.bfloat16)
        step_b.append(send(sb.at[s], rb.at[s], b_ss.at[s], b_rs.at[s], far_row(p), z))

    def stage_c(s):
        p, h = quarter(s)
        step_b[s].wait_recv()
        j = (1 - h) * (1 - y) + h * (1 - x)
        q = (1 - h) * (2 * j + x) + h * (2 * y + j)
        sc[s] = (own[s, q] + ra[s, q] + rb[s, j].astype(jnp.float32)).astype(jnp.bfloat16)
        step_c.append(send(sc.at[s], rc.at[s], c_ss.at[s], c_rs.at[s], near_row(p), z))

    def stage_d(s):
        p, h = quarter(s)
        step_c[s].wait_recv()
        j = (1 - h) * y + h * x
        done = own[s, corner] + ra[s, corner] + rb[s, j].astype(jnp.float32) + rc[s].astype(jnp.float32)
        if order[s] == 0:
            return done
        i = order[s] - 1
        sd[i] = done.astype(jnp.bfloat16)
        step_d.append(send(sd.at[i], rd.at[i], d_ss.at[i], d_rs.at[i], r, p))

    def input_rows(lo, hi):
        back = lax.dot_general(
            cg[PAD * lo : PAD * hi, :], w[...], (((1,), (1,)), ((), ())),
            preferred_element_type=jnp.float32,
        ).astype(jnp.bfloat16)
        for im in range(lo, hi):
            ig[im] = back[PAD * (im - lo) : PAD * (im - lo) + positions, :]

    stage_a(0)
    stage_a(1)
    stage_b(0)
    stage_a(2)
    stage_b(1)
    stage_c(0)
    stage_a(3)
    stage_b(2)
    stage_c(1)
    stage_d(0)
    stage_b(3)
    input_rows(0, images // 2)
    stage_c(2)
    stage_d(1)
    gather_base.far_out()
    stage_c(3)
    input_rows(images // 2, images)
    put(ig, ig_hbm)
    stage_d(2)
    grad = stage_d(3)
    for copy in step_d:
        copy.wait_recv()
    for i in range(n_col - 1):
        grad += rd[i].astype(jnp.float32)
    grad = grad * (1.0 / total_images)

    gsq = jnp.sum(grad * grad, axis=0, keepdims=True)
    g_part = functools.reduce(lambda p, q: p + q, [gsq[:, c : c + 128] for c in range(0, cblk, 128)])
    own_n1 = n1.at[r]
    own_n1[0:1, :] = g_part
    own_n1[1:2, :] = m_part
    norm1 = [
        send(n1.at[r], n1.at[r], n1_ss.at[j - 1], n1_rs.at[j - 1], row_peer(j), z) for j in range(1, n_row)
    ]
    gsum[block(r, z)] = grad.astype(jnp.bfloat16)
    gather_grad.along_col()
    for copy in norm1:
        copy.wait_recv()
    n2[z] = functools.reduce(lambda p, q: p + q, [n1[j] for j in range(n_row)])
    norm2 = [
        send(n2.at[z], n2.at[z], n2_ss.at[i - 1], n2_rs.at[i - 1], r, col_peer(i)) for i in range(1, n_col)
    ]
    gather_grad.own_out()
    for copy in norm2:
        copy.wait_recv()
    norm = functools.reduce(lambda p, q: p + q, [n2[i] for i in range(n_col)])
    gnorm = jnp.sqrt(jnp.sum(norm[0:1, :], axis=1, keepdims=True))
    wnorm = jnp.sqrt(jnp.sum(norm[1:2, :], axis=1, keepdims=True))
    trust = trust_coef * wnorm / (gnorm + weight_decay * wnorm)
    rate = learn_rate * trust
    gather_grad.near_out()
    weights_now = master_ref[...]
    new_velocity = momentum * velocity_ref[...] + rate * (grad + weight_decay * weights_now)
    nv_ref[...] = new_velocity
    nm_ref[...] = weights_now - new_velocity
    put(nv_ref, nv_hbm)
    put(nm_ref, nm_hbm)
    for copy in bns:
        copy.wait_recv()
    sums = functools.reduce(lambda p, q: p + q, [bn[j] for j in range(n_row)])
    new_bnv = momentum * bnv_ref[...] + learn_rate * (sums * (1.0 / total_images))
    nbv_ref[...] = new_bnv
    nbn_ref[...] = bn_ref[...] - new_bnv
    put(nbv_ref, nbv_hbm)
    put(nbn_ref, nbn_hbm)
    gather_grad.far_out()

    def update(row, p):
        at_block = block(row, p)
        low = w[at_block].astype(jnp.float32)
        change = base[at_block].astype(jnp.float32)
        step = rate * (gsum[at_block].astype(jnp.float32) + weight_decay * low)
        nw_ref[at_block] = (low + (change - step)).astype(jnp.bfloat16)

    for n in range(4):
        for i in range(n_col):
            gather_base.from_sibling(n, i)
    def put_rows(row):
        rows = pl.ds(pl.multiple_of(row * rblk, rblk), rblk)
        put(nw_ref.at[rows], nw_hbm.at[rows])

    for n in range(4):
        for i in range(n_col):
            update(gather_grad.rows(col_peer(i))[n], col_peer(i))
    for j in range(4):
        put_rows(2 * j + k)
    for n in range(4):
        for i in range(n_col):
            update(*gather_grad.from_sibling(n, i))
    for j in range(4):
        put_rows(2 * j + 1 - k)
    for copy in stats + bns + core + step_b + step_c + step_d + norm1 + norm2 + sends:
        copy.wait_send()
    for copy in writes:
        copy.wait()


def write_out(*refs):
    count = len(refs) // 3
    ins, outs, held = refs[:count], refs[count : 2 * count], refs[2 * count : 3 * count]
    in_sem, out_sem = refs[3 * count :]
    first = [pltpu.make_async_copy(ins[n], held[n], in_sem.at[n]) for n in range(count)]
    second = [pltpu.make_async_copy(held[n], outs[n], out_sem.at[n]) for n in range(count)]
    for copy in first:
        copy.start()
    for n in range(count):
        first[n].wait()
        second[n].start()
    for copy in second:
        copy.wait()


def fused(activations, pre_activation, pooled_grad, weights, master, velocity, bn_params, bn_velocity):
    images, positions, in_chan = activations.shape
    out_chan = weights.shape[1]
    rows = images * PAD
    rblk, cblk = master.shape
    f32, bf16 = jnp.float32, jnp.bfloat16
    hbm = pl.BlockSpec(memory_space=pltpu.HBM)
    dma = pltpu.SemaphoreType.DMA
    pairs = (12, 7, 4, 4, 4, 3, 7, 3, 32, 32)
    flops = 6 * images * positions * in_chan * out_chan
    args = (activations, pre_activation, pooled_grad, weights, master, velocity, bn_params, bn_velocity)
    shapes = tuple(
        jax.ShapeDtypeStruct(a.shape, a.dtype)
        for a in (activations, master, master, weights, bn_params, bn_params)
    )
    results = pl.pallas_call(
        kernel,
        out_shape=shapes,
        in_specs=[hbm] * len(args),
        out_specs=(hbm,) * len(shapes),
        scratch_shapes=[pltpu.VMEM(a.shape, a.dtype) for a in args + shapes]
        + [
            pltpu.VMEM((rows, in_chan), bf16),
            pltpu.VMEM((2, in_chan // 2, rows), bf16),
            pltpu.VMEM((rows, out_chan), bf16),
            pltpu.VMEM((rows, out_chan), bf16),
            pltpu.VMEM(pooled_grad.shape, f32),
            pltpu.VMEM(weights.shape, bf16),
            pltpu.VMEM(weights.shape, bf16),
            pltpu.VMEM((4, 4, 4, cblk), f32),
            pltpu.VMEM((8, 2, out_chan), f32),
            pltpu.VMEM((4, out_chan), f32),
            pltpu.VMEM((4, 4, rblk, cblk), f32),
            pltpu.VMEM((4, 4, rblk, cblk), f32),
            pltpu.VMEM((4, 4, rblk, cblk), f32),
            pltpu.VMEM((4, 2, rblk, cblk), bf16),
            pltpu.VMEM((4, 2, rblk, cblk), bf16),
            pltpu.VMEM((4, rblk, cblk), bf16),
            pltpu.VMEM((4, rblk, cblk), bf16),
            pltpu.VMEM((3, rblk, cblk), bf16),
            pltpu.VMEM((3, rblk, cblk), bf16),
            pltpu.VMEM((8, 2, 128), f32),
            pltpu.VMEM((4, 2, 128), f32),
            dma((8,)),
            dma((16,)),
        ]
        + [dma((n,)) for n in pairs for _ in range(2)],
        compiler_params=pltpu.CompilerParams(
            collective_id=0, has_side_effects=True, vmem_limit_bytes=LIMIT
        ),
        cost_estimate=pl.CostEstimate(flops=flops, bytes_accessed=8 * 1024 * 1024, transcendentals=0),
    )(*args)
    return pl.pallas_call(
        write_out,
        out_shape=shapes,
        in_specs=[hbm] * len(shapes),
        out_specs=(hbm,) * len(shapes),
        scratch_shapes=[pltpu.VMEM(a.shape, a.dtype) for a in shapes] + [dma((len(shapes),))] * 2,
        compiler_params=pltpu.CompilerParams(vmem_limit_bytes=LIMIT),
    )(*results)


def pick(mesh):
    if mesh.shape["row"] == 8 and mesh.shape["col"] == 4:
        return fused
    return body


def solution(mesh):
    placed = (
        P(("row", "col"), None, None),
        P(("row", "col"), None, None),
        P(("row", "col"), None),
        P(),
        P("row", "col"),
        P("row", "col"),
        P(),
        P(),
    )
    return jax.shard_map(
        pick(mesh),
        mesh=mesh,
        in_specs=placed,
        out_specs=(P(("row", "col"), None, None), P("row", "col"), P("row", "col"), P(), P(), P()),
        check_vma=False,
    )
```

```python
import functools

import jax
import jax.numpy as jnp
from jax import lax
from jax.experimental import pallas as pl
from jax.experimental.pallas import tpu as pltpu
from jax.sharding import PartitionSpec as P

epsilon = 1e-05
trust_coef = 0.001
weight_decay = 0.0001
momentum = 0.9
learn_rate = 12.0


def body(
    activations, pre_activation, pooled_grad, weights, master, velocity, bn_params, bn_velocity
):
    images, positions, in_chan = activations.shape
    out_chan = weights.shape[1]
    row_count = images * positions
    n_row = lax.axis_size("row")
    n_col = lax.axis_size("col")
    group_element_count = row_count * n_col
    total_images = images * n_row * n_col
    norm_scale_weight = bn_params[0]
    flat_in = activations.reshape(row_count, in_chan)
    conv_low = jnp.dot(flat_in, weights, preferred_element_type=jnp.float32).astype(jnp.bfloat16)
    expand_conv_output = lax.optimization_barrier(conv_low).astype(jnp.float32)
    stats = lax.psum(
        (
            jnp.sum(expand_conv_output, axis=0),
            jnp.sum(expand_conv_output * expand_conv_output, axis=0),
        ),
        "col",
    )
    group_mean_value = stats[0] / group_element_count
    variance = stats[1] / group_element_count - group_mean_value * group_mean_value
    inverse_deviation = lax.rsqrt(variance + epsilon)
    upstream_all = jnp.broadcast_to(
        (pooled_grad / positions)[:, None, :], pre_activation.shape
    ).reshape(row_count, out_chan)
    incoming_gradient = jnp.where(
        pre_activation.reshape(row_count, out_chan) > 0, upstream_all, jnp.zeros_like(upstream_all)
    )
    normalized_input = (expand_conv_output - group_mean_value) * inverse_deviation
    local_up = jnp.sum(incoming_gradient, axis=0)
    local_upstream_normalized = jnp.sum(incoming_gradient * normalized_input, axis=0)
    group_totals_reduced = lax.psum((local_up, local_upstream_normalized), "col")
    expand_conv_gradient = (
        norm_scale_weight
        * inverse_deviation
        * (
            incoming_gradient
            - group_totals_reduced[0] / group_element_count
            - normalized_input * group_totals_reduced[1] / group_element_count
        )
    ).astype(jnp.bfloat16)
    back = lax.dot_general(
        expand_conv_gradient, weights, (((1,), (1,)), ((), ())), preferred_element_type=jnp.float32
    )
    input_grad = back.astype(jnp.bfloat16).reshape(images, positions, in_chan)
    row_part = lax.psum_scatter(
        lax.dot_general(
            flat_in,
            expand_conv_gradient,
            (((0,), (0,)), ((), ())),
            preferred_element_type=jnp.float32,
        ),
        "row",
        scatter_dimension=0,
        tiled=True,
    )
    grad_sum = lax.psum_scatter(row_part, "col", scatter_dimension=1, tiled=True)
    weight_grad = grad_sum * (1.0 / total_images)
    master_sq = jnp.sum(master * master)
    grad_sq = jnp.sum(weight_grad * weight_grad)
    bn_tot = lax.psum((group_totals_reduced[1], group_totals_reduced[0]), "row")
    norms = lax.psum((master_sq, grad_sq), ("row", "col"))
    upx_total, up_total = (bn_tot[0], bn_tot[1])
    master_total, grad_total = (norms[0], norms[1])
    wnorm = jnp.sqrt(master_total)
    gnorm = jnp.sqrt(grad_total)
    trust = trust_coef * wnorm / (gnorm + weight_decay * wnorm)
    new_velocity = momentum * velocity + learn_rate * trust * (weight_grad + weight_decay * master)
    new_master = master - new_velocity
    shard_low = new_master.astype(jnp.bfloat16)
    wide_rows = lax.all_gather(shard_low, "col", axis=1, tiled=True)
    new_weights = lax.all_gather(wide_rows, "row", axis=0, tiled=True)
    bn_grad = jnp.stack([upx_total, up_total]) * (1.0 / total_images)
    new_bn_velocity = momentum * bn_velocity + learn_rate * bn_grad
    new_bn = bn_params - new_bn_velocity
    return (input_grad, new_master, new_velocity, new_weights, new_bn, new_bn_velocity)


MESH = pl.DeviceIdType.MESH
PAD = 64
LIMIT = 58 * 1024 * 1024


def flip(value, bit):
    return lax.rem(value + bit, 2)


def kernel(
    act_hbm, pre_hbm, pool_hbm, w_hbm, master_hbm, velocity_hbm, bn_hbm, bnv_hbm,
    ig_hbm, nm_hbm, nv_hbm, nw_hbm, nbn_hbm, nbv_hbm,
    act, pre, pool_ref, w, master_ref, velocity_ref, bn_ref, bnv_ref,
    ig, nm_ref, nv_ref, nw_ref, nbn_ref, nbv_ref,
    a_s, at, conv, cg, poolg, base, gsum,
    st, coef, sa, ra, own, sb, rb, sc, rc, sd, rd, n1, n2,
    in_sem, out_sem, st_ss, st_rs, a_ss, a_rs, b_ss, b_rs, c_ss, c_rs, d_ss, d_rs,
    n1_ss, n1_rs, n2_ss, n2_rs, base_ss, base_rs, gsum_ss, gsum_rs,
):
    images, positions, in_chan = act.shape
    out_chan = w.shape[1]
    n_row, n_col = 8, 4
    rblk, cblk = in_chan // n_row, out_chan // n_col
    device_count = images * positions
    count = device_count * n_col
    total_images = images * n_row * n_col
    r, z = lax.axis_index("row"), lax.axis_index("col")
    k, x, y = lax.rem(r, 2), lax.rem(r // 2, 2), r // 4

    def row_of(yy, xx, kk):
        return 4 * yy + 2 * xx + kk

    def row_peer(j):
        return row_of(flip(y, j // 4), flip(x, (j // 2) % 2), flip(k, j % 2))

    def col_peer(i):
        return 2 * flip(z // 2, i // 2) + flip(lax.rem(z, 2), i % 2)

    def send(src, dst, ss, rs, row, col):
        copy = pltpu.make_async_remote_copy(
            src_ref=src, dst_ref=dst, send_sem=ss, recv_sem=rs,
            device_id=(row, col), device_id_type=MESH,
        )
        copy.start()
        return copy

    barrier = pltpu.get_barrier_semaphore()
    for j in range(1, n_row):
        pl.semaphore_signal(barrier, inc=1, device_id=(row_peer(j), z), device_id_type=MESH)
    for i in range(1, n_col):
        pl.semaphore_signal(barrier, inc=1, device_id=(r, col_peer(i)), device_id_type=MESH)

    loads = [
        pltpu.make_async_copy(src, dst, in_sem.at[n])
        for n, (src, dst) in enumerate(
            (
                (master_hbm, master_ref),
                (velocity_hbm, velocity_ref),
                (w_hbm, w),
                (act_hbm, act),
                (pool_hbm, pool_ref),
                (pre_hbm, pre),
                (bn_hbm, bn_ref),
                (bnv_hbm, bnv_ref),
            )
        )
    ]
    for load in loads:
        load.start()

    sends, puts = [], []

    def put(src, dst):
        copy = pltpu.make_async_copy(src, dst, out_sem.at[len(puts)])
        copy.start()
        puts.append(copy)

    half = 2 * cblk

    def block(row, p, width):
        rows = pl.ds(pl.multiple_of(row * rblk, rblk), rblk)
        return rows, pl.ds(pl.multiple_of(p * width, width), width)

    def plane_row(n, h, core):
        n0, n1 = n % 2, n // 2
        return row_of(flip(y, n0 * (1 - h) + n1 * h), flip(x, n0 * h + n1 * (1 - h)), core)

    sibling = row_of(y, x, 1 - k)

    def piece(buf, ss, rs, where, slot, to_row, to_col):
        return pltpu.make_async_remote_copy(
            src_ref=buf.at[where], dst_ref=buf.at[where], send_sem=ss.at[slot], recv_sem=rs.at[slot],
            device_id=(to_row, to_col), device_id_type=MESH,
        )

    def along_col(buf, ss, rs):
        for i in range(1, n_col):
            copy = piece(buf, ss, rs, block(r, z, cblk), i, r, col_peer(i))
            copy.start()
            sends.append(copy)

    def arrived_col(buf, ss, rs, i):
        p = col_peer(i)
        piece(buf, ss, rs, block(r, p, cblk), i, r, p).wait_recv()

    def base_piece(n, slot, to_row, core=k):
        return piece(base, base_ss, base_rs, block(plane_row(n, 0, core), 0, out_chan), slot, to_row, z)

    def base_out():
        for i in range(1, n_col):
            arrived_col(base, base_ss, base_rs, i)
        for n in range(1, 4):
            copy = base_piece(0, 3 + n, plane_row(n, 0, k))
            copy.start()
            sends.append(copy)
        copy = base_piece(0, 7, sibling)
        copy.start()
        sends.append(copy)

    def base_relay():
        for n in range(1, 4):
            base_piece(n, 3 + n, plane_row(n, 0, k)).wait_recv()
            copy = base_piece(n, 7 + n, sibling)
            copy.start()
            sends.append(copy)

    def grad_piece(n, t, slot, to_row, core=k):
        h = flip(z // 2, t)
        return piece(gsum, gsum_ss, gsum_rs, block(plane_row(n, h, core), h, half), slot, to_row, z)

    def grad_send(n, t, slot, to):
        h = flip(z // 2, t)
        copy = grad_piece(n, t, slot, sibling if to == 0 else plane_row(to, h, k))
        copy.start()
        sends.append(copy)

    def grad_own_out():
        for t in range(2):
            for i in ((1,), (2, 3))[t]:
                arrived_col(gsum, gsum_ss, gsum_rs, i)
            grad_send(0, t, 4 + t, 1)
            grad_send(0, t, 6 + t, 2)
            grad_send(0, t, 10 + t, 0)

    def grad_near_out():
        for t in range(2):
            grad_piece(1, t, 4 + t, sibling).wait_recv()
            grad_send(1, t, 8 + t, 2)
            grad_send(1, t, 12 + t, 0)

    def grad_far_out():
        for t in range(2):
            grad_piece(2, t, 6 + t, sibling).wait_recv()
            grad_send(2, t, 14 + t, 0)
        for t in range(2):
            grad_piece(3, t, 8 + t, sibling).wait_recv()
            grad_send(3, t, 16 + t, 0)

    cg[...] = jnp.zeros_like(cg)
    a_s[...] = jnp.zeros_like(a_s)
    loads[0].wait()
    loads[1].wait()
    loads[2].wait()
    weights_now = master_ref[...]
    base[block(r, z, cblk)] = (
        weights_now - w[block(r, z, cblk)].astype(jnp.float32) - momentum * velocity_ref[...]
    ).astype(jnp.bfloat16)
    msq = jnp.sum(weights_now * weights_now, axis=0, keepdims=True)
    m_part = functools.reduce(lambda p, q: p + q, [msq[:, c : c + 128] for c in range(0, cblk, 128)])
    pl.semaphore_wait(barrier, n_row + n_col - 2)
    along_col(base, base_ss, base_rs)
    loads[3].wait()
    for im in range(images):
        a_s[PAD * im : PAD * im + positions, :] = act[im]
    loads[4].wait()
    poolg[...] = pool_ref[...] / positions
    loads[5].wait()

    @pl.loop(0, n_col)
    def conv_columns(part):
        cols = pl.ds(pl.multiple_of(part * cblk, cblk), cblk)
        own_st = st.at[z, part]
        low = jnp.dot(a_s[...], w[:, cols], preferred_element_type=jnp.float32).astype(jnp.bfloat16)
        conv[:, cols] = low
        wide = low.astype(jnp.float32)
        total = jnp.sum(wide, axis=0, keepdims=True)
        mean = total / device_count
        own_st[0:1, :] = total
        own_st[1:2, :] = jnp.sum(wide * wide, axis=0, keepdims=True)
        up_sum = jnp.zeros((1, cblk), jnp.float32)
        upx_sum = jnp.zeros((1, cblk), jnp.float32)
        for im in range(images):
            rows = conv[PAD * im : PAD * im + positions, cols].astype(jnp.float32)
            keep = pre[im, :, cols].astype(jnp.float32) > 0
            pooled = poolg[im : im + 1, cols]
            up_sum += pooled * jnp.sum(jnp.where(keep, 1.0, 0.0), axis=0, keepdims=True)
            upx_sum += pooled * jnp.sum(jnp.where(keep, rows - mean, 0.0), axis=0, keepdims=True)
        own_st[2:3, :] = up_sum
        own_st[3:4, :] = upx_sum


    stats = [
        send(st.at[z], st.at[z], st_ss.at[i - 1], st_rs.at[i - 1], r, col_peer(i)) for i in range(1, n_col)
    ]
    base_out()
    turned = a_s[...].T
    for q in range(n_row):
        at[q % 2, (q // 2) * rblk : (q // 2 + 1) * rblk, :] = turned[q * rblk : (q + 1) * rblk, :]
    for copy in stats:
        copy.wait_recv()
    parts = [jnp.concatenate([st[i, part] for part in range(n_col)], axis=1) for i in range(n_col)]
    mu = (parts[0][0:1] + parts[1][0:1] + parts[2][0:1] + parts[3][0:1]) / count
    square = parts[0][1:2] + parts[1][1:2] + parts[2][1:2] + parts[3][1:2]
    su = parts[0][2:3] + parts[1][2:3] + parts[2][2:3] + parts[3][2:3]
    rstd = lax.rsqrt(square / count - mu * mu + epsilon)
    sx = jnp.zeros_like(mu)
    for part in parts:
        sx += part[3:4] + (part[0:1] / device_count - mu) * part[2:3]
    sx = sx * rstd
    own_n1 = n1.at[r]
    own_n1[0:1, :out_chan] = sx
    own_n1[1:2, :out_chan] = su
    loads[6].wait()
    loads[7].wait()
    scale = bn_ref[0:1, :] * rstd
    coef[0:1, :] = scale
    coef[1:2, :] = scale * su / count
    coef[2:3, :] = scale * rstd * sx / count
    coef[3:4, :] = mu

    corner = 2 * y + x

    def quarter(s):
        i = 2 * (1 - s % 2) + 1 - s // 2
        p = 2 * flip(z // 2, 1 - s % 2) + flip(lax.rem(z, 2), 1 - s // 2)
        return i, p, p // 2

    def remote(src, dst, ss, rs, row, col):
        return pltpu.make_async_remote_copy(
            src_ref=src, dst_ref=dst, send_sem=ss, recv_sem=rs,
            device_id=(row, col), device_id_type=MESH,
        )

    def copy_a(s):
        return remote(sa.at[s], ra.at[s], a_ss.at[s], a_rs.at[s], sibling, z)

    def copy_b(s):
        return remote(sb.at[s], rb.at[s], b_ss.at[s], b_rs.at[s], plane_row(2, quarter(s)[2], k), z)

    def copy_c(s):
        return remote(sc.at[s], rc.at[s], c_ss.at[s], c_rs.at[s], plane_row(1, quarter(s)[2], k), z)

    def copy_d(s):
        i, p, _ = quarter(s)
        return remote(sd.at[s], rd.at[s], d_ss.at[s], d_rs.at[s], r, p)

    def stage_a(s):
        _, p, _ = quarter(s)
        cols = pl.ds(pl.multiple_of(p * cblk, cblk), cblk)
        scale_c, shift_c, slope_c, mu_c = (coef[n : n + 1, cols] for n in range(4))
        for im in range(images):
            span = slice(PAD * im, PAD * im + positions)
            rows = conv[span, cols].astype(jnp.float32)
            keep = pre[im, :, cols].astype(jnp.float32) > 0
            up = jnp.where(keep, scale_c * poolg[im : im + 1, cols], 0.0)
            cg[span, cols] = (up - shift_c - slope_c * (rows - mu_c)).astype(jnp.bfloat16)
        product = jnp.dot(at[1 - k], cg[:, cols], preferred_element_type=jnp.float32)
        sa[s] = product.reshape(4, rblk, cblk)
        copy_a(s).start()
        product = jnp.dot(at[k], cg[:, cols], preferred_element_type=jnp.float32)
        own[s] = product.reshape(4, rblk, cblk)

    def stage_b(s):
        _, _, h = quarter(s)
        copy_a(s).wait_recv()
        for j in range(2):
            q = (1 - h) * (2 * j + 1 - x) + h * (2 * (1 - y) + j)
            sb[s, j] = (own[s, q] + ra[s, q]).astype(jnp.bfloat16)
        copy_b(s).start()

    def stage_c(s):
        _, _, h = quarter(s)
        copy_b(s).wait_recv()
        j = (1 - h) * (1 - y) + h * (1 - x)
        q = (1 - h) * (2 * j + x) + h * (2 * y + j)
        sc[s] = (own[s, q] + ra[s, q] + rb[s, j].astype(jnp.float32)).astype(jnp.bfloat16)
        copy_c(s).start()

    def stage_d(s):
        _, _, h = quarter(s)
        copy_c(s).wait_recv()
        j = (1 - h) * y + h * x
        done = own[s, corner] + ra[s, corner] + rb[s, j].astype(jnp.float32) + rc[s].astype(jnp.float32)
        if isinstance(s, int) and s == 3:
            return done
        sd[s] = done.astype(jnp.bfloat16)
        copy_d(s).start()

    def input_rows(lo, hi):
        back = lax.dot_general(
            cg[PAD * lo : PAD * hi, :], w[...], (((1,), (1,)), ((), ())),
            preferred_element_type=jnp.float32,
        ).astype(jnp.bfloat16)
        for im in range(lo, hi):
            ig[im] = back[PAD * (im - lo) : PAD * (im - lo) + positions, :]

    @pl.loop(0, 4)
    def reduce_quarters(s):
        stage_a(s)
        pl.when(s >= 1)(lambda: stage_b(s - 1))
        pl.when(s >= 2)(lambda: stage_c(s - 2))

    stage_b(3)
    stage_d(0)
    input_rows(0, images // 2)
    stage_c(2)
    stage_d(1)
    base_relay()
    stage_c(3)
    input_rows(images // 2, images)
    put(ig, ig_hbm)
    stage_d(2)
    grad = stage_d(3)
    for i in range(n_col - 1):
        copy_d(i).wait_recv()
        grad += rd[i].astype(jnp.float32)
    grad = grad * (1.0 / total_images)

    gsq = jnp.sum(grad * grad, axis=0, keepdims=True)
    g_part = functools.reduce(lambda p, q: p + q, [gsq[:, c : c + 128] for c in range(0, cblk, 128)])
    own_n1[0:1, out_chan:] = g_part
    own_n1[1:2, out_chan:] = m_part
    norm1 = [
        send(n1.at[r], n1.at[r], n1_ss.at[j - 1], n1_rs.at[j - 1], row_peer(j), z) for j in range(1, n_row)
    ]
    gsum[block(r, z, cblk)] = grad.astype(jnp.bfloat16)
    along_col(gsum, gsum_ss, gsum_rs)
    for copy in norm1:
        copy.wait_recv()
    all_sums = functools.reduce(lambda p, q: p + q, [n1[j] for j in range(n_row)])
    n2[z] = all_sums[:, out_chan:]
    norm2 = [
        send(n2.at[z], n2.at[z], n2_ss.at[i - 1], n2_rs.at[i - 1], r, col_peer(i)) for i in range(1, n_col)
    ]
    grad_own_out()
    for copy in norm2:
        copy.wait_recv()
    norm = functools.reduce(lambda p, q: p + q, [n2[i] for i in range(n_col)])
    gnorm = jnp.sqrt(jnp.sum(norm[0:1, :], axis=1, keepdims=True))
    wnorm = jnp.sqrt(jnp.sum(norm[1:2, :], axis=1, keepdims=True))
    trust = trust_coef * wnorm / (gnorm + weight_decay * wnorm)
    rate = learn_rate * trust
    grad_near_out()
    weights_now = master_ref[...]
    new_velocity = momentum * velocity_ref[...] + rate * (grad + weight_decay * weights_now)
    nv_ref[...] = new_velocity
    nm_ref[...] = weights_now - new_velocity
    put(nv_ref, nv_hbm)
    put(nm_ref, nm_hbm)
    sums = all_sums[:, :out_chan]
    new_bnv = momentum * bnv_ref[...] + learn_rate * (sums * (1.0 / total_images))
    nbv_ref[...] = new_bnv
    nbn_ref[...] = bn_ref[...] - new_bnv
    put(nbv_ref, nbv_hbm)
    put(nbn_ref, nbn_hbm)
    grad_far_out()

    def update(at_block):
        low = w[at_block].astype(jnp.float32)
        change = base[at_block].astype(jnp.float32)
        step = rate * (gsum[at_block].astype(jnp.float32) + weight_decay * low)
        nw_ref[at_block] = (low + (change - step)).astype(jnp.bfloat16)

    @pl.loop(0, 8)
    def update_own(e):
        update(block(2 * (e // 2) + k, e % 2, half))

    for n in range(4):
        base_piece(n, 7 + n, sibling, 1 - k).wait_recv()

    @pl.loop(0, 8)
    def update_other(e):
        n, t = e // 2, e % 2
        grad_piece(n, t, 10 + e, sibling, 1 - k).wait_recv()
        h = flip(z // 2, t)
        update(block(plane_row(n, h, 1 - k), h, half))

    put(nw_ref, nw_hbm)
    for copy in stats + norm1 + norm2 + sends:
        copy.wait_send()
    for s in range(4):
        copy_a(s).wait_send()
        copy_b(s).wait_send()
        copy_c(s).wait_send()
        if s < 3:
            copy_d(s).wait_send()
    for copy in puts:
        copy.wait()


def write_out(*refs):
    count = len(refs) // 3
    ins, outs, held = refs[:count], refs[count : 2 * count], refs[2 * count : 3 * count]
    in_sem, out_sem = refs[3 * count :]
    first = [pltpu.make_async_copy(ins[n], held[n], in_sem.at[n]) for n in range(count)]
    second = [pltpu.make_async_copy(held[n], outs[n], out_sem.at[n]) for n in range(count)]
    for copy in first:
        copy.start()
    for n in range(count):
        first[n].wait()
        second[n].start()
    for copy in second:
        copy.wait()


def fused(activations, pre_activation, pooled_grad, weights, master, velocity, bn_params, bn_velocity):
    images, positions, in_chan = activations.shape
    out_chan = weights.shape[1]
    rows = images * PAD
    rblk, cblk = master.shape
    f32, bf16 = jnp.float32, jnp.bfloat16
    hbm = pl.BlockSpec(memory_space=pltpu.HBM)
    dma = pltpu.SemaphoreType.DMA
    pairs = (3, 4, 4, 4, 3, 7, 3, 11, 18)
    flops = 6 * images * positions * in_chan * out_chan
    args = (activations, pre_activation, pooled_grad, weights, master, velocity, bn_params, bn_velocity)
    shapes = tuple(
        jax.ShapeDtypeStruct(a.shape, a.dtype)
        for a in (activations, master, master, weights, bn_params, bn_params)
    )
    results = pl.pallas_call(
        kernel,
        out_shape=shapes,
        in_specs=[hbm] * len(args),
        out_specs=(hbm,) * len(shapes),
        scratch_shapes=[pltpu.VMEM(a.shape, a.dtype) for a in args + shapes]
        + [
            pltpu.VMEM((rows, in_chan), bf16),
            pltpu.VMEM((2, in_chan // 2, rows), bf16),
            pltpu.VMEM((rows, out_chan), bf16),
            pltpu.VMEM((rows, out_chan), bf16),
            pltpu.VMEM(pooled_grad.shape, f32),
            pltpu.VMEM(weights.shape, bf16),
            pltpu.VMEM(weights.shape, bf16),
            pltpu.VMEM((4, 4, 4, cblk), f32),
            pltpu.VMEM((4, out_chan), f32),
            pltpu.VMEM((4, 4, rblk, cblk), f32),
            pltpu.VMEM((4, 4, rblk, cblk), f32),
            pltpu.VMEM((4, 4, rblk, cblk), f32),
            pltpu.VMEM((4, 2, rblk, cblk), bf16),
            pltpu.VMEM((4, 2, rblk, cblk), bf16),
            pltpu.VMEM((4, rblk, cblk), bf16),
            pltpu.VMEM((4, rblk, cblk), bf16),
            pltpu.VMEM((3, rblk, cblk), bf16),
            pltpu.VMEM((3, rblk, cblk), bf16),
            pltpu.VMEM((8, 2, out_chan + 128), f32),
            pltpu.VMEM((4, 2, 128), f32),
            dma((8,)),
            dma((16,)),
        ]
        + [dma((n,)) for n in pairs for _ in range(2)],
        compiler_params=pltpu.CompilerParams(
            collective_id=0, has_side_effects=True, vmem_limit_bytes=LIMIT
        ),
        cost_estimate=pl.CostEstimate(flops=flops, bytes_accessed=8 * 1024 * 1024, transcendentals=0),
    )(*args)
    return pl.pallas_call(
        write_out,
        out_shape=shapes,
        in_specs=[hbm] * len(shapes),
        out_specs=(hbm,) * len(shapes),
        scratch_shapes=[pltpu.VMEM(a.shape, a.dtype) for a in shapes] + [dma((len(shapes),))] * 2,
        compiler_params=pltpu.CompilerParams(vmem_limit_bytes=LIMIT),
    )(*results)


def pick(mesh):
    if mesh.shape["row"] == 8 and mesh.shape["col"] == 4:
        return fused
    return body


def solution(mesh):
    placed = (
        P(("row", "col"), None, None),
        P(("row", "col"), None, None),
        P(("row", "col"), None),
        P(),
        P("row", "col"),
        P("row", "col"),
        P(),
        P(),
    )
    return jax.shard_map(
        pick(mesh),
        mesh=mesh,
        in_specs=placed,
        out_specs=(P(("row", "col"), None, None), P("row", "col"), P("row", "col"), P(), P(), P()),
        check_vma=False,
    )
```

```python
import functools

import jax
import jax.numpy as jnp
from jax import lax
from jax.experimental import pallas as pl
from jax.experimental.pallas import tpu as pltpu
from jax.sharding import PartitionSpec as P

epsilon = 1e-05
trust_coef = 0.001
weight_decay = 0.0001
momentum = 0.9
learn_rate = 12.0


def body(
    activations, pre_activation, pooled_grad, weights, master, velocity, bn_params, bn_velocity
):
    images, positions, in_chan = activations.shape
    out_chan = weights.shape[1]
    row_count = images * positions
    n_row = lax.axis_size("row")
    n_col = lax.axis_size("col")
    group_element_count = row_count * n_col
    total_images = images * n_row * n_col
    norm_scale_weight = bn_params[0]
    flat_in = activations.reshape(row_count, in_chan)
    conv_low = jnp.dot(flat_in, weights, preferred_element_type=jnp.float32).astype(jnp.bfloat16)
    expand_conv_output = lax.optimization_barrier(conv_low).astype(jnp.float32)
    stats = lax.psum(
        (
            jnp.sum(expand_conv_output, axis=0),
            jnp.sum(expand_conv_output * expand_conv_output, axis=0),
        ),
        "col",
    )
    group_mean_value = stats[0] / group_element_count
    variance = stats[1] / group_element_count - group_mean_value * group_mean_value
    inverse_deviation = lax.rsqrt(variance + epsilon)
    upstream_all = jnp.broadcast_to(
        (pooled_grad / positions)[:, None, :], pre_activation.shape
    ).reshape(row_count, out_chan)
    incoming_gradient = jnp.where(
        pre_activation.reshape(row_count, out_chan) > 0, upstream_all, jnp.zeros_like(upstream_all)
    )
    normalized_input = (expand_conv_output - group_mean_value) * inverse_deviation
    local_up = jnp.sum(incoming_gradient, axis=0)
    local_upstream_normalized = jnp.sum(incoming_gradient * normalized_input, axis=0)
    group_totals_reduced = lax.psum((local_up, local_upstream_normalized), "col")
    expand_conv_gradient = (
        norm_scale_weight
        * inverse_deviation
        * (
            incoming_gradient
            - group_totals_reduced[0] / group_element_count
            - normalized_input * group_totals_reduced[1] / group_element_count
        )
    ).astype(jnp.bfloat16)
    back = lax.dot_general(
        expand_conv_gradient, weights, (((1,), (1,)), ((), ())), preferred_element_type=jnp.float32
    )
    input_grad = back.astype(jnp.bfloat16).reshape(images, positions, in_chan)
    row_part = lax.psum_scatter(
        lax.dot_general(
            flat_in,
            expand_conv_gradient,
            (((0,), (0,)), ((), ())),
            preferred_element_type=jnp.float32,
        ),
        "row",
        scatter_dimension=0,
        tiled=True,
    )
    grad_sum = lax.psum_scatter(row_part, "col", scatter_dimension=1, tiled=True)
    weight_grad = grad_sum * (1.0 / total_images)
    master_sq = jnp.sum(master * master)
    grad_sq = jnp.sum(weight_grad * weight_grad)
    bn_tot = lax.psum((group_totals_reduced[1], group_totals_reduced[0]), "row")
    norms = lax.psum((master_sq, grad_sq), ("row", "col"))
    upx_total, up_total = (bn_tot[0], bn_tot[1])
    master_total, grad_total = (norms[0], norms[1])
    wnorm = jnp.sqrt(master_total)
    gnorm = jnp.sqrt(grad_total)
    trust = trust_coef * wnorm / (gnorm + weight_decay * wnorm)
    new_velocity = momentum * velocity + learn_rate * trust * (weight_grad + weight_decay * master)
    new_master = master - new_velocity
    shard_low = new_master.astype(jnp.bfloat16)
    wide_rows = lax.all_gather(shard_low, "col", axis=1, tiled=True)
    new_weights = lax.all_gather(wide_rows, "row", axis=0, tiled=True)
    bn_grad = jnp.stack([upx_total, up_total]) * (1.0 / total_images)
    new_bn_velocity = momentum * bn_velocity + learn_rate * bn_grad
    new_bn = bn_params - new_bn_velocity
    return (input_grad, new_master, new_velocity, new_weights, new_bn, new_bn_velocity)


MESH = pl.DeviceIdType.MESH
PAD = 64
LIMIT = 58 * 1024 * 1024


def flip(value, bit):
    return lax.rem(value + bit, 2)


def kernel(
    act_hbm, pre_hbm, pool_hbm, w_hbm, master_hbm, velocity_hbm, bn_hbm, bnv_hbm,
    ig_hbm, nm_hbm, nv_hbm, nw_hbm, nbn_hbm, nbv_hbm,
    act, pre, pool_ref, w, master_ref, velocity_ref, bn_ref, bnv_ref,
    ig, nm_ref, nv_ref, nw_ref, nbn_ref, nbv_ref,
    a_s, at, conv, cg, poolg, base, gsum,
    st, coef, sa, ra, own, sb, rb, sc, rc, sd, rd, n1, n2,
    in_sem, out_sem, st_ss, st_rs, a_ss, a_rs, b_ss, b_rs, c_ss, c_rs, d_ss, d_rs,
    n1_ss, n1_rs, n2_ss, n2_rs, base_ss, base_rs, gsum_ss, gsum_rs,
):
    images, positions, in_chan = act.shape
    out_chan = w.shape[1]
    n_row, n_col = 8, 4
    rblk, cblk = in_chan // n_row, out_chan // n_col
    device_count = images * positions
    count = device_count * n_col
    total_images = images * n_row * n_col
    r, z = lax.axis_index("row"), lax.axis_index("col")
    k, x, y = lax.rem(r, 2), lax.rem(r // 2, 2), r // 4

    def row_of(yy, xx, kk):
        return 4 * yy + 2 * xx + kk

    def row_peer(j):
        return row_of(flip(y, j // 4), flip(x, (j // 2) % 2), flip(k, j % 2))

    def col_peer(i):
        return 2 * flip(z // 2, i // 2) + flip(lax.rem(z, 2), i % 2)

    def send(src, dst, ss, rs, row, col):
        copy = pltpu.make_async_remote_copy(
            src_ref=src, dst_ref=dst, send_sem=ss, recv_sem=rs,
            device_id=(row, col), device_id_type=MESH,
        )
        copy.start()
        return copy

    barrier = pltpu.get_barrier_semaphore()
    for j in range(1, n_row):
        pl.semaphore_signal(barrier, inc=1, device_id=(row_peer(j), z), device_id_type=MESH)
    for i in range(1, n_col):
        pl.semaphore_signal(barrier, inc=1, device_id=(r, col_peer(i)), device_id_type=MESH)

    loads = [
        pltpu.make_async_copy(src, dst, in_sem.at[n])
        for n, (src, dst) in enumerate(
            (
                (master_hbm, master_ref),
                (velocity_hbm, velocity_ref),
                (w_hbm, w),
                (act_hbm, act),
                (pool_hbm, pool_ref),
                (pre_hbm, pre),
                (bn_hbm, bn_ref),
                (bnv_hbm, bnv_ref),
            )
        )
    ]
    for load in loads:
        load.start()

    sends, puts = [], []

    def put(src, dst):
        copy = pltpu.make_async_copy(src, dst, out_sem.at[len(puts)])
        copy.start()
        puts.append(copy)

    half = 2 * cblk

    def block(row, p, width):
        rows = pl.ds(pl.multiple_of(row * rblk, rblk), rblk)
        return rows, pl.ds(pl.multiple_of(p * width, width), width)

    def plane_row(n, h, core):
        n0, n1 = n % 2, n // 2
        return row_of(flip(y, n0 * (1 - h) + n1 * h), flip(x, n0 * h + n1 * (1 - h)), core)

    sibling = row_of(y, x, 1 - k)

    def piece(buf, ss, rs, where, slot, to_row, to_col):
        return pltpu.make_async_remote_copy(
            src_ref=buf.at[where], dst_ref=buf.at[where], send_sem=ss.at[slot], recv_sem=rs.at[slot],
            device_id=(to_row, to_col), device_id_type=MESH,
        )

    def along_col(buf, ss, rs):
        for i in range(1, n_col):
            copy = piece(buf, ss, rs, block(r, z, cblk), i, r, col_peer(i))
            copy.start()
            sends.append(copy)

    def arrived_col(buf, ss, rs, i):
        p = col_peer(i)
        piece(buf, ss, rs, block(r, p, cblk), i, r, p).wait_recv()

    def base_piece(n, slot, to_row, core=k):
        return piece(base, base_ss, base_rs, block(plane_row(n, 0, core), 0, out_chan), slot, to_row, z)

    def base_out():
        for i in range(1, n_col):
            arrived_col(base, base_ss, base_rs, i)
        for n in range(1, 4):
            copy = base_piece(0, 3 + n, plane_row(n, 0, k))
            copy.start()
            sends.append(copy)
        copy = base_piece(0, 7, sibling)
        copy.start()
        sends.append(copy)

    def base_relay():
        for n in range(1, 4):
            base_piece(n, 3 + n, plane_row(n, 0, k)).wait_recv()
            copy = base_piece(n, 7 + n, sibling)
            copy.start()
            sends.append(copy)

    def grad_piece(n, t, slot, to_row, core=k):
        h = flip(z // 2, t)
        return piece(gsum, gsum_ss, gsum_rs, block(plane_row(n, h, core), h, half), slot, to_row, z)

    def grad_send(n, t, slot, to):
        h = flip(z // 2, t)
        copy = grad_piece(n, t, slot, sibling if to == 0 else plane_row(to, h, k))
        copy.start()
        sends.append(copy)

    def grad_own_out(t):
        for i in ((1,), (2, 3))[t]:
            arrived_col(gsum, gsum_ss, gsum_rs, i)
        grad_send(0, t, 4 + t, 1)
        grad_send(0, t, 6 + t, 2)
        grad_send(0, t, 10 + t, 0)

    def grad_near_out():
        for t in range(2):
            grad_piece(1, t, 4 + t, sibling).wait_recv()
            grad_send(1, t, 8 + t, 2)
            grad_send(1, t, 12 + t, 0)

    def grad_far_out():
        for t in range(2):
            grad_piece(2, t, 6 + t, sibling).wait_recv()
            grad_send(2, t, 14 + t, 0)
        for t in range(2):
            grad_piece(3, t, 8 + t, sibling).wait_recv()
            grad_send(3, t, 16 + t, 0)

    cg[...] = jnp.zeros_like(cg)
    a_s[...] = jnp.zeros_like(a_s)
    loads[0].wait()
    loads[1].wait()
    loads[2].wait()
    weights_now = master_ref[...]
    base[block(r, z, cblk)] = (
        weights_now - w[block(r, z, cblk)].astype(jnp.float32) - momentum * velocity_ref[...]
    ).astype(jnp.bfloat16)
    msq = jnp.sum(weights_now * weights_now, axis=0, keepdims=True)
    m_part = functools.reduce(lambda p, q: p + q, [msq[:, c : c + 128] for c in range(0, cblk, 128)])
    pl.semaphore_wait(barrier, n_row + n_col - 2)
    along_col(base, base_ss, base_rs)
    loads[3].wait()
    for im in range(images):
        a_s[PAD * im : PAD * im + positions, :] = act[im]
    loads[4].wait()
    poolg[...] = pool_ref[...] / positions
    loads[5].wait()

    def conv_columns(part):
        cols = pl.ds(pl.multiple_of(part * cblk, cblk), cblk)
        own_st = st.at[z, part]
        low = jnp.dot(a_s[...], w[:, cols], preferred_element_type=jnp.float32).astype(jnp.bfloat16)
        conv[:, cols] = low
        wide = low.astype(jnp.float32)
        total = jnp.sum(wide, axis=0, keepdims=True)
        mean = total / device_count
        own_st[0:1, :] = total
        own_st[1:2, :] = jnp.sum(wide * wide, axis=0, keepdims=True)
        up_sum = jnp.zeros((1, cblk), jnp.float32)
        upx_sum = jnp.zeros((1, cblk), jnp.float32)
        for im in range(images):
            rows = conv[PAD * im : PAD * im + positions, cols].astype(jnp.float32)
            keep = pre[im, :, cols].astype(jnp.float32) > 0
            pooled = poolg[im : im + 1, cols]
            up_sum += pooled * jnp.sum(jnp.where(keep, 1.0, 0.0), axis=0, keepdims=True)
            upx_sum += pooled * jnp.sum(jnp.where(keep, rows - mean, 0.0), axis=0, keepdims=True)
        own_st[2:3, :] = up_sum
        own_st[3:4, :] = upx_sum

    pl.loop(0, 2)(conv_columns)
    base_out()
    pl.loop(2, n_col)(conv_columns)
    stats = [
        send(st.at[z], st.at[z], st_ss.at[i - 1], st_rs.at[i - 1], r, col_peer(i)) for i in range(1, n_col)
    ]
    turned = a_s[...].T
    for q in range(n_row):
        at[q % 2, (q // 2) * rblk : (q // 2 + 1) * rblk, :] = turned[q * rblk : (q + 1) * rblk, :]
    for copy in stats:
        copy.wait_recv()
    parts = [jnp.concatenate([st[i, part] for part in range(n_col)], axis=1) for i in range(n_col)]
    mu = (parts[0][0:1] + parts[1][0:1] + parts[2][0:1] + parts[3][0:1]) / count
    square = parts[0][1:2] + parts[1][1:2] + parts[2][1:2] + parts[3][1:2]
    su = parts[0][2:3] + parts[1][2:3] + parts[2][2:3] + parts[3][2:3]
    rstd = lax.rsqrt(square / count - mu * mu + epsilon)
    sx = jnp.zeros_like(mu)
    for part in parts:
        sx += part[3:4] + (part[0:1] / device_count - mu) * part[2:3]
    sx = sx * rstd
    own_n1 = n1.at[r]
    own_n1[0:1, :out_chan] = sx
    own_n1[1:2, :out_chan] = su
    loads[6].wait()
    loads[7].wait()
    scale = bn_ref[0:1, :] * rstd
    coef[0:1, :] = scale
    coef[1:2, :] = scale * su / count
    coef[2:3, :] = scale * rstd * sx / count
    coef[3:4, :] = mu

    corner = 2 * y + x

    def quarter(s):
        i = 2 * (1 - s % 2) + 1 - s // 2
        p = 2 * flip(z // 2, 1 - s % 2) + flip(lax.rem(z, 2), 1 - s // 2)
        return i, p, p // 2

    def remote(src, dst, ss, rs, row, col):
        return pltpu.make_async_remote_copy(
            src_ref=src, dst_ref=dst, send_sem=ss, recv_sem=rs,
            device_id=(row, col), device_id_type=MESH,
        )

    def copy_a(s):
        return remote(sa.at[s], ra.at[s], a_ss.at[s], a_rs.at[s], sibling, z)

    def copy_b(s):
        return remote(sb.at[s], rb.at[s], b_ss.at[s], b_rs.at[s], plane_row(2, quarter(s)[2], k), z)

    def copy_c(s):
        return remote(sc.at[s], rc.at[s], c_ss.at[s], c_rs.at[s], plane_row(1, quarter(s)[2], k), z)

    def copy_d(s):
        i, p, _ = quarter(s)
        return remote(sd.at[s], rd.at[s], d_ss.at[s], d_rs.at[s], r, p)

    def stage_a(s):
        _, p, _ = quarter(s)
        cols = pl.ds(pl.multiple_of(p * cblk, cblk), cblk)
        scale_c, shift_c, slope_c, mu_c = (coef[n : n + 1, cols] for n in range(4))
        for im in range(images):
            span = slice(PAD * im, PAD * im + positions)
            rows = conv[span, cols].astype(jnp.float32)
            keep = pre[im, :, cols].astype(jnp.float32) > 0
            up = jnp.where(keep, scale_c * poolg[im : im + 1, cols], 0.0)
            cg[span, cols] = (up - shift_c - slope_c * (rows - mu_c)).astype(jnp.bfloat16)
        both = at[...].reshape(in_chan, images * PAD)
        product = jnp.dot(both, cg[:, cols], preferred_element_type=jnp.float32)
        own[s] = product.reshape(2, 4, rblk, cblk)
        sa[s] = own[s, 1 - k].astype(jnp.bfloat16)
        copy_a(s).start()

    def stage_b(s):
        _, _, h = quarter(s)
        copy_a(s).wait_recv()
        for j in range(2):
            q = (1 - h) * (2 * j + 1 - x) + h * (2 * (1 - y) + j)
            sb[s, j] = (own[s, k, q] + ra[s, q].astype(jnp.float32)).astype(jnp.bfloat16)
        copy_b(s).start()

    def stage_c(s):
        _, _, h = quarter(s)
        copy_b(s).wait_recv()
        j = (1 - h) * (1 - y) + h * (1 - x)
        q = (1 - h) * (2 * j + x) + h * (2 * y + j)
        sc[s] = (own[s, k, q] + ra[s, q].astype(jnp.float32) + rb[s, j].astype(jnp.float32)).astype(jnp.bfloat16)
        copy_c(s).start()

    def stage_d(s):
        _, _, h = quarter(s)
        copy_c(s).wait_recv()
        j = (1 - h) * y + h * x
        done = own[s, k, corner] + ra[s, corner].astype(jnp.float32) + rb[s, j].astype(jnp.float32) + rc[s].astype(jnp.float32)
        if isinstance(s, int) and s == 3:
            return done
        sd[s] = done.astype(jnp.bfloat16)
        copy_d(s).start()

    def input_rows(lo, hi):
        back = lax.dot_general(
            cg[PAD * lo : PAD * hi, :], w[...], (((1,), (1,)), ((), ())),
            preferred_element_type=jnp.float32,
        ).astype(jnp.bfloat16)
        for im in range(lo, hi):
            ig[im] = back[PAD * (im - lo) : PAD * (im - lo) + positions, :]

    @pl.loop(0, 4)
    def reduce_quarters(s):
        stage_a(s)
        pl.when(s >= 1)(lambda: stage_b(s - 1))
        pl.when(s >= 2)(lambda: stage_c(s - 2))

    stage_b(3)
    stage_d(0)
    stage_c(2)
    stage_d(1)
    stage_c(3)
    base_relay()
    stage_d(2)
    input_rows(0, images // 2)
    grad = stage_d(3)
    for i in range(n_col - 1):
        copy_d(i).wait_recv()
        grad += rd[i].astype(jnp.float32)
    grad = grad * (1.0 / total_images)

    gsq = jnp.sum(grad * grad, axis=0, keepdims=True)
    g_part = functools.reduce(lambda p, q: p + q, [gsq[:, c : c + 128] for c in range(0, cblk, 128)])
    own_n1[0:1, out_chan:] = g_part
    own_n1[1:2, out_chan:] = m_part
    norm1 = [
        send(n1.at[r], n1.at[r], n1_ss.at[j - 1], n1_rs.at[j - 1], row_peer(j), z) for j in range(1, n_row)
    ]
    gsum[block(r, z, cblk)] = grad.astype(jnp.bfloat16)
    along_col(gsum, gsum_ss, gsum_rs)
    input_rows(images // 2, images)
    put(ig, ig_hbm)
    grad_own_out(0)
    for copy in norm1:
        copy.wait_recv()
    all_sums = functools.reduce(lambda p, q: p + q, [n1[j] for j in range(n_row)])
    n2[z] = all_sums[:, out_chan:]
    norm2 = [
        send(n2.at[z], n2.at[z], n2_ss.at[i - 1], n2_rs.at[i - 1], r, col_peer(i)) for i in range(1, n_col)
    ]
    grad_own_out(1)
    sums = all_sums[:, :out_chan]
    new_bnv = momentum * bnv_ref[...] + learn_rate * (sums * (1.0 / total_images))
    nbv_ref[...] = new_bnv
    nbn_ref[...] = bn_ref[...] - new_bnv
    put(nbv_ref, nbv_hbm)
    put(nbn_ref, nbn_hbm)
    grad_near_out()
    for copy in norm2:
        copy.wait_recv()
    norm = functools.reduce(lambda p, q: p + q, [n2[i] for i in range(n_col)])
    gnorm = jnp.sqrt(jnp.sum(norm[0:1, :], axis=1, keepdims=True))
    wnorm = jnp.sqrt(jnp.sum(norm[1:2, :], axis=1, keepdims=True))
    trust = trust_coef * wnorm / (gnorm + weight_decay * wnorm)
    rate = learn_rate * trust
    weights_now = master_ref[...]
    new_velocity = momentum * velocity_ref[...] + rate * (grad + weight_decay * weights_now)
    nv_ref[...] = new_velocity
    nm_ref[...] = weights_now - new_velocity
    put(nv_ref, nv_hbm)
    put(nm_ref, nm_hbm)
    grad_far_out()

    def update(at_block):
        low = w[at_block].astype(jnp.float32)
        change = base[at_block].astype(jnp.float32)
        step = rate * (gsum[at_block].astype(jnp.float32) + weight_decay * low)
        nw_ref[at_block] = (low + (change - step)).astype(jnp.bfloat16)

    @pl.loop(0, 8)
    def update_own(e):
        update(block(2 * (e // 2) + k, e % 2, half))

    for n in range(4):
        base_piece(n, 7 + n, sibling, 1 - k).wait_recv()

    @pl.loop(0, 8)
    def update_other(e):
        n, t = e // 2, e % 2
        grad_piece(n, t, 10 + e, sibling, 1 - k).wait_recv()
        h = flip(z // 2, t)
        update(block(plane_row(n, h, 1 - k), h, half))

    put(nw_ref, nw_hbm)
    for copy in stats + norm1 + norm2 + sends:
        copy.wait_send()
    for s in range(4):
        copy_a(s).wait_send()
        copy_b(s).wait_send()
        copy_c(s).wait_send()
        if s < 3:
            copy_d(s).wait_send()
    for copy in puts:
        copy.wait()


def write_out(*refs):
    count = len(refs) // 3
    ins, outs, held = refs[:count], refs[count : 2 * count], refs[2 * count : 3 * count]
    in_sem, out_sem = refs[3 * count :]
    moves = []
    for n in range(count):
        size = ins[n].shape[0]
        pieces = 4 if size % 64 == 0 and ins[n].dtype == jnp.bfloat16 else 1
        step = size // pieces
        for part in range(pieces):
            rows = pl.ds(part * step, step)
            moves.append((ins[n].at[rows], held[n].at[rows], outs[n].at[rows]))
    first = [pltpu.make_async_copy(a, b, in_sem.at[m]) for m, (a, b, _) in enumerate(moves)]
    second = [pltpu.make_async_copy(b, c, out_sem.at[m]) for m, (_, b, c) in enumerate(moves)]
    for copy in first:
        copy.start()
    for m in range(len(moves)):
        first[m].wait()
        second[m].start()
    for copy in second:
        copy.wait()


def fused(activations, pre_activation, pooled_grad, weights, master, velocity, bn_params, bn_velocity):
    images, positions, in_chan = activations.shape
    out_chan = weights.shape[1]
    rows = images * PAD
    rblk, cblk = master.shape
    f32, bf16 = jnp.float32, jnp.bfloat16
    hbm = pl.BlockSpec(memory_space=pltpu.HBM)
    dma = pltpu.SemaphoreType.DMA
    pairs = (3, 4, 4, 4, 3, 7, 3, 11, 18)
    flops = 6 * images * positions * in_chan * out_chan
    args = (activations, pre_activation, pooled_grad, weights, master, velocity, bn_params, bn_velocity)
    shapes = tuple(
        jax.ShapeDtypeStruct(a.shape, a.dtype)
        for a in (activations, master, master, weights, bn_params, bn_params)
    )
    results = pl.pallas_call(
        kernel,
        out_shape=shapes,
        in_specs=[hbm] * len(args),
        out_specs=(hbm,) * len(shapes),
        scratch_shapes=[pltpu.VMEM(a.shape, a.dtype) for a in args + shapes]
        + [
            pltpu.VMEM((rows, in_chan), bf16),
            pltpu.VMEM((2, in_chan // 2, rows), bf16),
            pltpu.VMEM((rows, out_chan), bf16),
            pltpu.VMEM((rows, out_chan), bf16),
            pltpu.VMEM(pooled_grad.shape, f32),
            pltpu.VMEM(weights.shape, bf16),
            pltpu.VMEM(weights.shape, bf16),
            pltpu.VMEM((4, 4, 4, cblk), f32),
            pltpu.VMEM((4, out_chan), f32),
            pltpu.VMEM((4, 4, rblk, cblk), bf16),
            pltpu.VMEM((4, 4, rblk, cblk), bf16),
            pltpu.VMEM((4, 2, 4, rblk, cblk), f32),
            pltpu.VMEM((4, 2, rblk, cblk), bf16),
            pltpu.VMEM((4, 2, rblk, cblk), bf16),
            pltpu.VMEM((4, rblk, cblk), bf16),
            pltpu.VMEM((4, rblk, cblk), bf16),
            pltpu.VMEM((3, rblk, cblk), bf16),
            pltpu.VMEM((3, rblk, cblk), bf16),
            pltpu.VMEM((8, 2, out_chan + 128), f32),
            pltpu.VMEM((4, 2, 128), f32),
            dma((8,)),
            dma((16,)),
        ]
        + [dma((n,)) for n in pairs for _ in range(2)],
        compiler_params=pltpu.CompilerParams(
            collective_id=0, has_side_effects=True, vmem_limit_bytes=LIMIT
        ),
        cost_estimate=pl.CostEstimate(flops=flops, bytes_accessed=8 * 1024 * 1024, transcendentals=0),
    )(*args)
    return pl.pallas_call(
        write_out,
        out_shape=shapes,
        in_specs=[hbm] * len(shapes),
        out_specs=(hbm,) * len(shapes),
        scratch_shapes=[pltpu.VMEM(a.shape, a.dtype) for a in shapes] + [dma((16,))] * 2,
        compiler_params=pltpu.CompilerParams(vmem_limit_bytes=LIMIT),
    )(*results)


def pick(mesh):
    if mesh.shape["row"] == 8 and mesh.shape["col"] == 4:
        return fused
    return body


def solution(mesh):
    placed = (
        P(("row", "col"), None, None),
        P(("row", "col"), None, None),
        P(("row", "col"), None),
        P(),
        P("row", "col"),
        P("row", "col"),
        P(),
        P(),
    )
    return jax.shard_map(
        pick(mesh),
        mesh=mesh,
        in_specs=placed,
        out_specs=(P(("row", "col"), None, None), P("row", "col"), P("row", "col"), P(), P(), P()),
        check_vma=False,
    )
```

```python
import functools

import jax
import jax.numpy as jnp
from jax import lax
from jax.experimental import pallas as pl
from jax.experimental.pallas import tpu as pltpu
from jax.sharding import PartitionSpec as P

epsilon = 1e-05
trust_coef = 0.001
weight_decay = 0.0001
momentum = 0.9
learn_rate = 12.0


def body(
    activations, pre_activation, pooled_grad, weights, master, velocity, bn_params, bn_velocity
):
    images, positions, in_chan = activations.shape
    out_chan = weights.shape[1]
    row_count = images * positions
    n_row = lax.axis_size("row")
    n_col = lax.axis_size("col")
    group_element_count = row_count * n_col
    total_images = images * n_row * n_col
    norm_scale_weight = bn_params[0]
    flat_in = activations.reshape(row_count, in_chan)
    conv_low = jnp.dot(flat_in, weights, preferred_element_type=jnp.float32).astype(jnp.bfloat16)
    expand_conv_output = lax.optimization_barrier(conv_low).astype(jnp.float32)
    stats = lax.psum(
        (
            jnp.sum(expand_conv_output, axis=0),
            jnp.sum(expand_conv_output * expand_conv_output, axis=0),
        ),
        "col",
    )
    group_mean_value = stats[0] / group_element_count
    variance = stats[1] / group_element_count - group_mean_value * group_mean_value
    inverse_deviation = lax.rsqrt(variance + epsilon)
    upstream_all = jnp.broadcast_to(
        (pooled_grad / positions)[:, None, :], pre_activation.shape
    ).reshape(row_count, out_chan)
    incoming_gradient = jnp.where(
        pre_activation.reshape(row_count, out_chan) > 0, upstream_all, jnp.zeros_like(upstream_all)
    )
    normalized_input = (expand_conv_output - group_mean_value) * inverse_deviation
    local_up = jnp.sum(incoming_gradient, axis=0)
    local_upstream_normalized = jnp.sum(incoming_gradient * normalized_input, axis=0)
    group_totals_reduced = lax.psum((local_up, local_upstream_normalized), "col")
    expand_conv_gradient = (
        norm_scale_weight
        * inverse_deviation
        * (
            incoming_gradient
            - group_totals_reduced[0] / group_element_count
            - normalized_input * group_totals_reduced[1] / group_element_count
        )
    ).astype(jnp.bfloat16)
    back = lax.dot_general(
        expand_conv_gradient, weights, (((1,), (1,)), ((), ())), preferred_element_type=jnp.float32
    )
    input_grad = back.astype(jnp.bfloat16).reshape(images, positions, in_chan)
    row_part = lax.psum_scatter(
        lax.dot_general(
            flat_in,
            expand_conv_gradient,
            (((0,), (0,)), ((), ())),
            preferred_element_type=jnp.float32,
        ),
        "row",
        scatter_dimension=0,
        tiled=True,
    )
    grad_sum = lax.psum_scatter(row_part, "col", scatter_dimension=1, tiled=True)
    weight_grad = grad_sum * (1.0 / total_images)
    master_sq = jnp.sum(master * master)
    grad_sq = jnp.sum(weight_grad * weight_grad)
    bn_tot = lax.psum((group_totals_reduced[1], group_totals_reduced[0]), "row")
    norms = lax.psum((master_sq, grad_sq), ("row", "col"))
    upx_total, up_total = (bn_tot[0], bn_tot[1])
    master_total, grad_total = (norms[0], norms[1])
    wnorm = jnp.sqrt(master_total)
    gnorm = jnp.sqrt(grad_total)
    trust = trust_coef * wnorm / (gnorm + weight_decay * wnorm)
    new_velocity = momentum * velocity + learn_rate * trust * (weight_grad + weight_decay * master)
    new_master = master - new_velocity
    shard_low = new_master.astype(jnp.bfloat16)
    wide_rows = lax.all_gather(shard_low, "col", axis=1, tiled=True)
    new_weights = lax.all_gather(wide_rows, "row", axis=0, tiled=True)
    bn_grad = jnp.stack([upx_total, up_total]) * (1.0 / total_images)
    new_bn_velocity = momentum * bn_velocity + learn_rate * bn_grad
    new_bn = bn_params - new_bn_velocity
    return (input_grad, new_master, new_velocity, new_weights, new_bn, new_bn_velocity)


MESH = pl.DeviceIdType.MESH
PAD = 64
LIMIT = 58 * 1024 * 1024


def flip(value, bit):
    return lax.rem(value + bit, 2)


def kernel(
    act_hbm, pre_hbm, pool_hbm, w_hbm, master_hbm, velocity_hbm, bn_hbm, bnv_hbm,
    ig_hbm, nm_hbm, nv_hbm, nw_hbm, nbn_hbm, nbv_hbm,
    act, pre, pool_ref, w, master_ref, velocity_ref, bn_ref, bnv_ref,
    ig, nm_ref, nv_ref, nw_ref, nbn_ref, nbv_ref,
    a_s, at, conv, cg, poolg, base, gsum,
    st, coef, sa, ra, own, sb, rb, sc, rc, sd, rd, n1, n2,
    in_sem, out_sem, st_ss, st_rs, a_ss, a_rs, b_ss, b_rs, c_ss, c_rs, d_ss, d_rs,
    n1_ss, n1_rs, n2_ss, n2_rs, base_ss, base_rs, gsum_ss, gsum_rs,
):
    images, positions, in_chan = act.shape
    out_chan = w.shape[1]
    n_row, n_col = 8, 4
    rblk, cblk = in_chan // n_row, out_chan // n_col
    device_count = images * positions
    count = device_count * n_col
    total_images = images * n_row * n_col
    r, z = lax.axis_index("row"), lax.axis_index("col")
    k, x, y = lax.rem(r, 2), lax.rem(r // 2, 2), r // 4

    def row_of(yy, xx, kk):
        return 4 * yy + 2 * xx + kk

    def row_peer(j):
        return row_of(flip(y, j // 4), flip(x, (j // 2) % 2), flip(k, j % 2))

    def col_peer(i):
        return 2 * flip(z // 2, i // 2) + flip(lax.rem(z, 2), i % 2)

    def send(src, dst, ss, rs, row, col):
        copy = pltpu.make_async_remote_copy(
            src_ref=src, dst_ref=dst, send_sem=ss, recv_sem=rs,
            device_id=(row, col), device_id_type=MESH,
        )
        copy.start()
        return copy

    barrier = pltpu.get_barrier_semaphore()
    for j in range(1, n_row):
        pl.semaphore_signal(barrier, inc=1, device_id=(row_peer(j), z), device_id_type=MESH)
    for i in range(1, n_col):
        pl.semaphore_signal(barrier, inc=1, device_id=(r, col_peer(i)), device_id_type=MESH)

    loads = [
        pltpu.make_async_copy(src, dst, in_sem.at[n])
        for n, (src, dst) in enumerate(
            (
                (master_hbm, master_ref),
                (velocity_hbm, velocity_ref),
                (w_hbm, w),
                (act_hbm, act),
                (pool_hbm, pool_ref),
                (pre_hbm, pre),
                (bn_hbm, bn_ref),
                (bnv_hbm, bnv_ref),
            )
        )
    ]
    for load in loads:
        load.start()

    sends, puts = [], []

    def put(src, dst):
        copy = pltpu.make_async_copy(src, dst, out_sem.at[len(puts)])
        copy.start()
        puts.append(copy)

    half = 2 * cblk

    def block(row, p, width):
        rows = pl.ds(pl.multiple_of(row * rblk, rblk), rblk)
        return rows, pl.ds(pl.multiple_of(p * width, width), width)

    def plane_row(n, h, core):
        n0, n1 = n % 2, n // 2
        return row_of(flip(y, n0 * (1 - h) + n1 * h), flip(x, n0 * h + n1 * (1 - h)), core)

    sibling = row_of(y, x, 1 - k)

    def piece(buf, ss, rs, where, slot, to_row, to_col):
        return pltpu.make_async_remote_copy(
            src_ref=buf.at[where], dst_ref=buf.at[where], send_sem=ss.at[slot], recv_sem=rs.at[slot],
            device_id=(to_row, to_col), device_id_type=MESH,
        )

    def along_col(buf, ss, rs):
        for i in range(1, n_col):
            copy = piece(buf, ss, rs, block(r, z, cblk), i, r, col_peer(i))
            copy.start()
            sends.append(copy)

    def arrived_col(buf, ss, rs, i):
        p = col_peer(i)
        piece(buf, ss, rs, block(r, p, cblk), i, r, p).wait_recv()

    def base_piece(n, slot, to_row, core=k):
        return piece(base, base_ss, base_rs, block(plane_row(n, 0, core), 0, out_chan), slot, to_row, z)

    def base_out():
        for i in range(1, n_col):
            arrived_col(base, base_ss, base_rs, i)
        for n in range(1, 4):
            copy = base_piece(0, 3 + n, plane_row(n, 0, k))
            copy.start()
            sends.append(copy)
        copy = base_piece(0, 7, sibling)
        copy.start()
        sends.append(copy)

    def base_relay():
        for n in range(1, 4):
            base_piece(n, 3 + n, plane_row(n, 0, k)).wait_recv()
            copy = base_piece(n, 7 + n, sibling)
            copy.start()
            sends.append(copy)

    def grad_piece(n, t, slot, to_row, core=k):
        h = flip(z // 2, t)
        return piece(gsum, gsum_ss, gsum_rs, block(plane_row(n, h, core), h, half), slot, to_row, z)

    def grad_send(n, t, slot, to):
        h = flip(z // 2, t)
        copy = grad_piece(n, t, slot, sibling if to == 0 else plane_row(to, h, k))
        copy.start()
        sends.append(copy)

    def grad_own_out(t):
        for i in ((1,), (2, 3))[t]:
            arrived_col(gsum, gsum_ss, gsum_rs, i)
        grad_send(0, t, 4 + t, 1)
        grad_send(0, t, 6 + t, 2)
        grad_send(0, t, 10 + t, 0)

    def grad_near_out():
        for t in range(2):
            grad_piece(1, t, 4 + t, sibling).wait_recv()
            grad_send(1, t, 8 + t, 2)
            grad_send(1, t, 12 + t, 0)

    def grad_far_out():
        for t in range(2):
            grad_piece(2, t, 6 + t, sibling).wait_recv()
            grad_send(2, t, 14 + t, 0)
        for t in range(2):
            grad_piece(3, t, 8 + t, sibling).wait_recv()
            grad_send(3, t, 16 + t, 0)

    cg[...] = jnp.zeros_like(cg)
    a_s[...] = jnp.zeros_like(a_s)
    loads[0].wait()
    loads[1].wait()
    loads[2].wait()
    weights_now = master_ref[...]
    base[block(r, z, cblk)] = (
        weights_now - w[block(r, z, cblk)].astype(jnp.float32) - momentum * velocity_ref[...]
    ).astype(jnp.bfloat16)
    msq = jnp.sum(weights_now * weights_now, axis=0, keepdims=True)
    m_part = functools.reduce(lambda p, q: p + q, [msq[:, c : c + 128] for c in range(0, cblk, 128)])
    pl.semaphore_wait(barrier, n_row + n_col - 2)
    along_col(base, base_ss, base_rs)
    loads[3].wait()
    for im in range(images):
        a_s[PAD * im : PAD * im + positions, :] = act[im]
    loads[4].wait()
    poolg[...] = pool_ref[...] / positions
    loads[5].wait()

    def conv_columns(part):
        cols = pl.ds(pl.multiple_of(part * cblk, cblk), cblk)
        own_st = st.at[z, part]
        low = jnp.dot(a_s[...], w[:, cols], preferred_element_type=jnp.float32).astype(jnp.bfloat16)
        conv[:, cols] = low
        wide = low.astype(jnp.float32)
        total = jnp.sum(wide, axis=0, keepdims=True)
        mean = total / device_count
        own_st[0:1, :] = total
        own_st[1:2, :] = jnp.sum(wide * wide, axis=0, keepdims=True)
        up_sum = jnp.zeros((1, cblk), jnp.float32)
        upx_sum = jnp.zeros((1, cblk), jnp.float32)
        for im in range(images):
            rows = conv[PAD * im : PAD * im + positions, cols].astype(jnp.float32)
            keep = pre[im, :, cols].astype(jnp.float32) > 0
            pooled = poolg[im : im + 1, cols]
            up_sum += pooled * jnp.sum(jnp.where(keep, 1.0, 0.0), axis=0, keepdims=True)
            upx_sum += pooled * jnp.sum(jnp.where(keep, rows - mean, 0.0), axis=0, keepdims=True)
        own_st[2:3, :] = up_sum
        own_st[3:4, :] = upx_sum

    pl.loop(0, n_col)(conv_columns)
    stats = [
        send(st.at[z], st.at[z], st_ss.at[i - 1], st_rs.at[i - 1], r, col_peer(i)) for i in range(1, n_col)
    ]
    turned = a_s[...].T
    for q in range(n_row):
        at[q % 2, (q // 2) * rblk : (q // 2 + 1) * rblk, :] = turned[q * rblk : (q + 1) * rblk, :]
    base_out()
    for copy in stats:
        copy.wait_recv()
    parts = [jnp.concatenate([st[i, part] for part in range(n_col)], axis=1) for i in range(n_col)]
    mu = (parts[0][0:1] + parts[1][0:1] + parts[2][0:1] + parts[3][0:1]) / count
    square = parts[0][1:2] + parts[1][1:2] + parts[2][1:2] + parts[3][1:2]
    su = parts[0][2:3] + parts[1][2:3] + parts[2][2:3] + parts[3][2:3]
    rstd = lax.rsqrt(square / count - mu * mu + epsilon)
    sx = jnp.zeros_like(mu)
    for part in parts:
        sx += part[3:4] + (part[0:1] / device_count - mu) * part[2:3]
    sx = sx * rstd
    own_n1 = n1.at[r]
    own_n1[0:1, :out_chan] = sx
    own_n1[1:2, :out_chan] = su
    loads[6].wait()
    loads[7].wait()
    scale = bn_ref[0:1, :] * rstd
    coef[0:1, :] = scale
    coef[1:2, :] = scale * su / count
    coef[2:3, :] = scale * rstd * sx / count
    coef[3:4, :] = mu

    corner = 2 * y + x

    def quarter(s):
        i = 2 * (1 - s % 2) + 1 - s // 2
        p = 2 * flip(z // 2, 1 - s % 2) + flip(lax.rem(z, 2), 1 - s // 2)
        return i, p, p // 2

    def remote(src, dst, ss, rs, row, col):
        return pltpu.make_async_remote_copy(
            src_ref=src, dst_ref=dst, send_sem=ss, recv_sem=rs,
            device_id=(row, col), device_id_type=MESH,
        )

    def copy_a(s):
        return remote(sa.at[s], ra.at[s], a_ss.at[s], a_rs.at[s], sibling, z)

    def copy_b(s):
        return remote(sb.at[s], rb.at[s], b_ss.at[s], b_rs.at[s], plane_row(2, quarter(s)[2], k), z)

    def copy_c(s):
        return remote(sc.at[s], rc.at[s], c_ss.at[s], c_rs.at[s], plane_row(1, quarter(s)[2], k), z)

    def copy_d(s):
        i, p, _ = quarter(s)
        return remote(sd.at[s], rd.at[s], d_ss.at[s], d_rs.at[s], r, p)

    def stage_a(s):
        _, p, _ = quarter(s)
        cols = pl.ds(pl.multiple_of(p * cblk, cblk), cblk)
        scale_c, shift_c, slope_c, mu_c = (coef[n : n + 1, cols] for n in range(4))
        for im in range(images):
            span = slice(PAD * im, PAD * im + positions)
            rows = conv[span, cols].astype(jnp.float32)
            keep = pre[im, :, cols].astype(jnp.float32) > 0
            up = jnp.where(keep, scale_c * poolg[im : im + 1, cols], 0.0)
            cg[span, cols] = (up - shift_c - slope_c * (rows - mu_c)).astype(jnp.bfloat16)
        both = at[...].reshape(in_chan, images * PAD)
        product = jnp.dot(both, cg[:, cols], preferred_element_type=jnp.float32)
        own[s] = product.reshape(2, 4, rblk, cblk)
        sa[s] = own[s, 1 - k].astype(jnp.bfloat16)
        copy_a(s).start()

    def stage_b(s):
        _, _, h = quarter(s)
        copy_a(s).wait_recv()
        for j in range(2):
            q = (1 - h) * (2 * j + 1 - x) + h * (2 * (1 - y) + j)
            sb[s, j] = (own[s, k, q] + ra[s, q].astype(jnp.float32)).astype(jnp.bfloat16)
        copy_b(s).start()

    def stage_c(s):
        _, _, h = quarter(s)
        copy_b(s).wait_recv()
        j = (1 - h) * (1 - y) + h * (1 - x)
        q = (1 - h) * (2 * j + x) + h * (2 * y + j)
        sc[s] = (own[s, k, q] + ra[s, q].astype(jnp.float32) + rb[s, j].astype(jnp.float32)).astype(jnp.bfloat16)
        copy_c(s).start()

    def stage_d(s):
        _, _, h = quarter(s)
        copy_c(s).wait_recv()
        j = (1 - h) * y + h * x
        done = own[s, k, corner] + ra[s, corner].astype(jnp.float32) + rb[s, j].astype(jnp.float32) + rc[s].astype(jnp.float32)
        if isinstance(s, int) and s == 3:
            return done
        sd[s] = done.astype(jnp.bfloat16)
        copy_d(s).start()

    def input_rows(lo, hi):
        back = lax.dot_general(
            cg[PAD * lo : PAD * hi, :], w[...], (((1,), (1,)), ((), ())),
            preferred_element_type=jnp.float32,
        ).astype(jnp.bfloat16)
        for im in range(lo, hi):
            ig[im] = back[PAD * (im - lo) : PAD * (im - lo) + positions, :]

    @pl.loop(0, 4)
    def reduce_quarters(s):
        stage_a(s)
        pl.when(s >= 1)(lambda: stage_b(s - 1))
        pl.when(s >= 2)(lambda: stage_c(s - 2))

    stage_b(3)
    stage_d(0)
    input_rows(0, images // 2)
    stage_c(2)
    stage_d(1)
    base_relay()
    stage_c(3)
    input_rows(images // 2, images)
    put(ig, ig_hbm)
    stage_d(2)
    grad = stage_d(3)
    for i in range(n_col - 1):
        copy_d(i).wait_recv()
        grad += rd[i].astype(jnp.float32)
    grad = grad * (1.0 / total_images)

    gsq = jnp.sum(grad * grad, axis=0, keepdims=True)
    g_part = functools.reduce(lambda p, q: p + q, [gsq[:, c : c + 128] for c in range(0, cblk, 128)])
    own_n1[0:1, out_chan:] = g_part
    own_n1[1:2, out_chan:] = m_part
    norm1 = [
        send(n1.at[r], n1.at[r], n1_ss.at[j - 1], n1_rs.at[j - 1], row_peer(j), z) for j in range(1, n_row)
    ]
    gsum[block(r, z, cblk)] = grad.astype(jnp.bfloat16)
    along_col(gsum, gsum_ss, gsum_rs)
    grad_own_out(0)
    for copy in norm1:
        copy.wait_recv()
    all_sums = functools.reduce(lambda p, q: p + q, [n1[j] for j in range(n_row)])
    n2[z] = all_sums[:, out_chan:]
    norm2 = [
        send(n2.at[z], n2.at[z], n2_ss.at[i - 1], n2_rs.at[i - 1], r, col_peer(i)) for i in range(1, n_col)
    ]
    grad_own_out(1)
    sums = all_sums[:, :out_chan]
    new_bnv = momentum * bnv_ref[...] + learn_rate * (sums * (1.0 / total_images))
    nbv_ref[...] = new_bnv
    nbn_ref[...] = bn_ref[...] - new_bnv
    put(nbv_ref, nbv_hbm)
    put(nbn_ref, nbn_hbm)
    grad_near_out()
    for copy in norm2:
        copy.wait_recv()
    norm = functools.reduce(lambda p, q: p + q, [n2[i] for i in range(n_col)])
    gnorm = jnp.sqrt(jnp.sum(norm[0:1, :], axis=1, keepdims=True))
    wnorm = jnp.sqrt(jnp.sum(norm[1:2, :], axis=1, keepdims=True))
    trust = trust_coef * wnorm / (gnorm + weight_decay * wnorm)
    rate = learn_rate * trust
    weights_now = master_ref[...]
    new_velocity = momentum * velocity_ref[...] + rate * (grad + weight_decay * weights_now)
    nv_ref[...] = new_velocity
    nm_ref[...] = weights_now - new_velocity
    put(nv_ref, nv_hbm)
    put(nm_ref, nm_hbm)
    grad_far_out()

    def update(at_block):
        low = w[at_block].astype(jnp.float32)
        change = base[at_block].astype(jnp.float32)
        step = rate * (gsum[at_block].astype(jnp.float32) + weight_decay * low)
        nw_ref[at_block] = (low + (change - step)).astype(jnp.bfloat16)

    @pl.loop(0, 8)
    def update_own(e):
        update(block(2 * (e // 2) + k, e % 2, half))

    for n in range(4):
        base_piece(n, 7 + n, sibling, 1 - k).wait_recv()

    @pl.loop(0, 8)
    def update_other(e):
        n, t = e // 2, e % 2
        grad_piece(n, t, 10 + e, sibling, 1 - k).wait_recv()
        h = flip(z // 2, t)
        update(block(plane_row(n, h, 1 - k), h, half))

    put(nw_ref, nw_hbm)
    for copy in stats + norm1 + norm2 + sends:
        copy.wait_send()
    for s in range(4):
        copy_a(s).wait_send()
        copy_b(s).wait_send()
        copy_c(s).wait_send()
        if s < 3:
            copy_d(s).wait_send()
    for copy in puts:
        copy.wait()


def write_out(*refs):
    count = len(refs) // 3
    ins, outs, held = refs[:count], refs[count : 2 * count], refs[2 * count : 3 * count]
    in_sem, out_sem = refs[3 * count :]
    first = [pltpu.make_async_copy(ins[n], held[n], in_sem.at[n]) for n in range(count)]
    second = [pltpu.make_async_copy(held[n], outs[n], out_sem.at[n]) for n in range(count)]
    for copy in first:
        copy.start()
    for n in range(count):
        first[n].wait()
        second[n].start()
    for copy in second:
        copy.wait()


def fused(activations, pre_activation, pooled_grad, weights, master, velocity, bn_params, bn_velocity):
    images, positions, in_chan = activations.shape
    out_chan = weights.shape[1]
    rows = images * PAD
    rblk, cblk = master.shape
    f32, bf16 = jnp.float32, jnp.bfloat16
    hbm = pl.BlockSpec(memory_space=pltpu.HBM)
    dma = pltpu.SemaphoreType.DMA
    pairs = (3, 4, 4, 4, 3, 7, 3, 11, 18)
    flops = 6 * images * positions * in_chan * out_chan
    args = (activations, pre_activation, pooled_grad, weights, master, velocity, bn_params, bn_velocity)
    shapes = tuple(
        jax.ShapeDtypeStruct(a.shape, a.dtype)
        for a in (activations, master, master, weights, bn_params, bn_params)
    )
    results = pl.pallas_call(
        kernel,
        out_shape=shapes,
        in_specs=[hbm] * len(args),
        out_specs=(hbm,) * len(shapes),
        scratch_shapes=[pltpu.VMEM(a.shape, a.dtype) for a in args + shapes]
        + [
            pltpu.VMEM((rows, in_chan), bf16),
            pltpu.VMEM((2, in_chan // 2, rows), bf16),
            pltpu.VMEM((rows, out_chan), bf16),
            pltpu.VMEM((rows, out_chan), bf16),
            pltpu.VMEM(pooled_grad.shape, f32),
            pltpu.VMEM(weights.shape, bf16),
            pltpu.VMEM(weights.shape, bf16),
            pltpu.VMEM((4, 4, 4, cblk), f32),
            pltpu.VMEM((4, out_chan), f32),
            pltpu.VMEM((4, 4, rblk, cblk), bf16),
            pltpu.VMEM((4, 4, rblk, cblk), bf16),
            pltpu.VMEM((4, 2, 4, rblk, cblk), f32),
            pltpu.VMEM((4, 2, rblk, cblk), bf16),
            pltpu.VMEM((4, 2, rblk, cblk), bf16),
            pltpu.VMEM((4, rblk, cblk), bf16),
            pltpu.VMEM((4, rblk, cblk), bf16),
            pltpu.VMEM((3, rblk, cblk), bf16),
            pltpu.VMEM((3, rblk, cblk), bf16),
            pltpu.VMEM((8, 2, out_chan + 128), f32),
            pltpu.VMEM((4, 2, 128), f32),
            dma((8,)),
            dma((16,)),
        ]
        + [dma((n,)) for n in pairs for _ in range(2)],
        compiler_params=pltpu.CompilerParams(
            collective_id=0, has_side_effects=True, vmem_limit_bytes=LIMIT
        ),
        cost_estimate=pl.CostEstimate(flops=flops, bytes_accessed=8 * 1024 * 1024, transcendentals=0),
    )(*args)
    return pl.pallas_call(
        write_out,
        out_shape=shapes,
        in_specs=[hbm] * len(shapes),
        out_specs=(hbm,) * len(shapes),
        scratch_shapes=[pltpu.VMEM(a.shape, a.dtype) for a in shapes] + [dma((len(shapes),))] * 2,
        compiler_params=pltpu.CompilerParams(vmem_limit_bytes=LIMIT),
    )(*results)


def pick(mesh):
    if mesh.shape["row"] == 8 and mesh.shape["col"] == 4:
        return fused
    return body


def solution(mesh):
    placed = (
        P(("row", "col"), None, None),
        P(("row", "col"), None, None),
        P(("row", "col"), None),
        P(),
        P("row", "col"),
        P("row", "col"),
        P(),
        P(),
    )
    return jax.shard_map(
        pick(mesh),
        mesh=mesh,
        in_specs=placed,
        out_specs=(P(("row", "col"), None, None), P("row", "col"), P("row", "col"), P(), P(), P()),
        check_vma=False,
    )
```

```python
import functools

import jax
import jax.numpy as jnp
from jax import lax
from jax.experimental import pallas as pl
from jax.experimental.pallas import tpu as pltpu
from jax.sharding import PartitionSpec as P

epsilon = 1e-05
trust_coef = 0.001
weight_decay = 0.0001
momentum = 0.9
learn_rate = 12.0


def body(
    activations, pre_activation, pooled_grad, weights, master, velocity, bn_params, bn_velocity
):
    images, positions, in_chan = activations.shape
    out_chan = weights.shape[1]
    row_count = images * positions
    n_row = lax.axis_size("row")
    n_col = lax.axis_size("col")
    group_element_count = row_count * n_col
    total_images = images * n_row * n_col
    norm_scale_weight = bn_params[0]
    flat_in = activations.reshape(row_count, in_chan)
    conv_low = jnp.dot(flat_in, weights, preferred_element_type=jnp.float32).astype(jnp.bfloat16)
    expand_conv_output = lax.optimization_barrier(conv_low).astype(jnp.float32)
    stats = lax.psum(
        (
            jnp.sum(expand_conv_output, axis=0),
            jnp.sum(expand_conv_output * expand_conv_output, axis=0),
        ),
        "col",
    )
    group_mean_value = stats[0] / group_element_count
    variance = stats[1] / group_element_count - group_mean_value * group_mean_value
    inverse_deviation = lax.rsqrt(variance + epsilon)
    upstream_all = jnp.broadcast_to(
        (pooled_grad / positions)[:, None, :], pre_activation.shape
    ).reshape(row_count, out_chan)
    incoming_gradient = jnp.where(
        pre_activation.reshape(row_count, out_chan) > 0, upstream_all, jnp.zeros_like(upstream_all)
    )
    normalized_input = (expand_conv_output - group_mean_value) * inverse_deviation
    local_up = jnp.sum(incoming_gradient, axis=0)
    local_upstream_normalized = jnp.sum(incoming_gradient * normalized_input, axis=0)
    group_totals_reduced = lax.psum((local_up, local_upstream_normalized), "col")
    expand_conv_gradient = (
        norm_scale_weight
        * inverse_deviation
        * (
            incoming_gradient
            - group_totals_reduced[0] / group_element_count
            - normalized_input * group_totals_reduced[1] / group_element_count
        )
    ).astype(jnp.bfloat16)
    back = lax.dot_general(
        expand_conv_gradient, weights, (((1,), (1,)), ((), ())), preferred_element_type=jnp.float32
    )
    input_grad = back.astype(jnp.bfloat16).reshape(images, positions, in_chan)
    row_part = lax.psum_scatter(
        lax.dot_general(
            flat_in,
            expand_conv_gradient,
            (((0,), (0,)), ((), ())),
            preferred_element_type=jnp.float32,
        ),
        "row",
        scatter_dimension=0,
        tiled=True,
    )
    grad_sum = lax.psum_scatter(row_part, "col", scatter_dimension=1, tiled=True)
    weight_grad = grad_sum * (1.0 / total_images)
    master_sq = jnp.sum(master * master)
    grad_sq = jnp.sum(weight_grad * weight_grad)
    bn_tot = lax.psum((group_totals_reduced[1], group_totals_reduced[0]), "row")
    norms = lax.psum((master_sq, grad_sq), ("row", "col"))
    upx_total, up_total = (bn_tot[0], bn_tot[1])
    master_total, grad_total = (norms[0], norms[1])
    wnorm = jnp.sqrt(master_total)
    gnorm = jnp.sqrt(grad_total)
    trust = trust_coef * wnorm / (gnorm + weight_decay * wnorm)
    new_velocity = momentum * velocity + learn_rate * trust * (weight_grad + weight_decay * master)
    new_master = master - new_velocity
    shard_low = new_master.astype(jnp.bfloat16)
    wide_rows = lax.all_gather(shard_low, "col", axis=1, tiled=True)
    new_weights = lax.all_gather(wide_rows, "row", axis=0, tiled=True)
    bn_grad = jnp.stack([upx_total, up_total]) * (1.0 / total_images)
    new_bn_velocity = momentum * bn_velocity + learn_rate * bn_grad
    new_bn = bn_params - new_bn_velocity
    return (input_grad, new_master, new_velocity, new_weights, new_bn, new_bn_velocity)


MESH = pl.DeviceIdType.MESH
PAD = 64
LIMIT = 58 * 1024 * 1024


def flip(value, bit):
    return lax.rem(value + bit, 2)


def kernel(
    act_hbm, pre_hbm, pool_hbm, w_hbm, master_hbm, velocity_hbm, bn_hbm, bnv_hbm,
    ig_hbm, nm_hbm, nv_hbm, nw_hbm, nbn_hbm, nbv_hbm,
    act, pre, pool_ref, w, master_ref, velocity_ref, bn_ref, bnv_ref,
    ig, nm_ref, nv_ref, nw_ref, nbn_ref, nbv_ref,
    a_s, at, conv, cg, poolg, base, gsum,
    st, coef, sa, ra, own, sb, rb, sc, rc, sd, rd, n1, n2,
    in_sem, out_sem, st_ss, st_rs, a_ss, a_rs, b_ss, b_rs, c_ss, c_rs, d_ss, d_rs,
    n1_ss, n1_rs, n2_ss, n2_rs, base_ss, base_rs, gsum_ss, gsum_rs,
):
    images, positions, in_chan = act.shape
    out_chan = w.shape[1]
    n_row, n_col = 8, 4
    rblk, cblk = in_chan // n_row, out_chan // n_col
    device_count = images * positions
    count = device_count * n_col
    total_images = images * n_row * n_col
    r, z = lax.axis_index("row"), lax.axis_index("col")
    k, x, y = lax.rem(r, 2), lax.rem(r // 2, 2), r // 4

    def row_of(yy, xx, kk):
        return 4 * yy + 2 * xx + kk

    def row_peer(j):
        return row_of(flip(y, j // 4), flip(x, (j // 2) % 2), flip(k, j % 2))

    def col_peer(i):
        return 2 * flip(z // 2, i // 2) + flip(lax.rem(z, 2), i % 2)

    def send(src, dst, ss, rs, row, col):
        copy = pltpu.make_async_remote_copy(
            src_ref=src, dst_ref=dst, send_sem=ss, recv_sem=rs,
            device_id=(row, col), device_id_type=MESH,
        )
        copy.start()
        return copy

    barrier = pltpu.get_barrier_semaphore()
    for j in range(1, n_row):
        pl.semaphore_signal(barrier, inc=1, device_id=(row_peer(j), z), device_id_type=MESH)
    for i in range(1, n_col):
        pl.semaphore_signal(barrier, inc=1, device_id=(r, col_peer(i)), device_id_type=MESH)

    loads = [
        pltpu.make_async_copy(src, dst, in_sem.at[n])
        for n, (src, dst) in enumerate(
            (
                (master_hbm, master_ref),
                (velocity_hbm, velocity_ref),
                (w_hbm, w),
                (act_hbm, act),
                (pool_hbm, pool_ref),
                (pre_hbm, pre),
                (bn_hbm, bn_ref),
                (bnv_hbm, bnv_ref),
            )
        )
    ]
    for load in loads:
        load.start()

    sends, puts = [], []

    def put(src, dst):
        copy = pltpu.make_async_copy(src, dst, out_sem.at[len(puts)])
        copy.start()
        puts.append(copy)

    half = 2 * cblk

    def block(row, p, width):
        rows = pl.ds(pl.multiple_of(row * rblk, rblk), rblk)
        return rows, pl.ds(pl.multiple_of(p * width, width), width)

    def plane_row(n, h, core):
        n0, n1 = n % 2, n // 2
        return row_of(flip(y, n0 * (1 - h) + n1 * h), flip(x, n0 * h + n1 * (1 - h)), core)

    sibling = row_of(y, x, 1 - k)

    def piece(buf, ss, rs, where, slot, to_row, to_col):
        return pltpu.make_async_remote_copy(
            src_ref=buf.at[where], dst_ref=buf.at[where], send_sem=ss.at[slot], recv_sem=rs.at[slot],
            device_id=(to_row, to_col), device_id_type=MESH,
        )

    def along_col(buf, ss, rs):
        for i in range(1, n_col):
            copy = piece(buf, ss, rs, block(r, z, cblk), i, r, col_peer(i))
            copy.start()
            sends.append(copy)

    def arrived_col(buf, ss, rs, i):
        p = col_peer(i)
        piece(buf, ss, rs, block(r, p, cblk), i, r, p).wait_recv()

    def base_piece(n, slot, to_row, core=k):
        return piece(base, base_ss, base_rs, block(plane_row(n, 0, core), 0, out_chan), slot, to_row, z)

    def base_out():
        for i in range(1, n_col):
            arrived_col(base, base_ss, base_rs, i)
        for n in range(1, 4):
            copy = base_piece(0, 3 + n, plane_row(n, 0, k))
            copy.start()
            sends.append(copy)
        copy = base_piece(0, 7, sibling)
        copy.start()
        sends.append(copy)

    def base_relay():
        for n in range(1, 4):
            base_piece(n, 3 + n, plane_row(n, 0, k)).wait_recv()
            copy = base_piece(n, 7 + n, sibling)
            copy.start()
            sends.append(copy)

    def grad_piece(n, t, slot, to_row, core=k):
        h = flip(z // 2, t)
        return piece(gsum, gsum_ss, gsum_rs, block(plane_row(n, h, core), h, half), slot, to_row, z)

    def grad_send(n, t, slot, to):
        h = flip(z // 2, t)
        copy = grad_piece(n, t, slot, sibling if to == 0 else plane_row(to, h, k))
        copy.start()
        sends.append(copy)

    def grad_own_out(t):
        for i in ((1,), (2, 3))[t]:
            arrived_col(gsum, gsum_ss, gsum_rs, i)
        grad_send(0, t, 4 + t, 1)
        grad_send(0, t, 6 + t, 2)
        grad_send(0, t, 10 + t, 0)

    def grad_near_out():
        for t in range(2):
            grad_piece(1, t, 4 + t, sibling).wait_recv()
            grad_send(1, t, 8 + t, 2)
            grad_send(1, t, 12 + t, 0)

    def grad_far_out():
        for t in range(2):
            grad_piece(2, t, 6 + t, sibling).wait_recv()
            grad_send(2, t, 14 + t, 0)
        for t in range(2):
            grad_piece(3, t, 8 + t, sibling).wait_recv()
            grad_send(3, t, 16 + t, 0)

    cg[...] = jnp.zeros_like(cg)
    a_s[...] = jnp.zeros_like(a_s)
    loads[0].wait()
    loads[1].wait()
    loads[2].wait()
    weights_now = master_ref[...]
    base[block(r, z, cblk)] = (
        weights_now - w[block(r, z, cblk)].astype(jnp.float32) - momentum * velocity_ref[...]
    ).astype(jnp.bfloat16)
    msq = jnp.sum(weights_now * weights_now, axis=0, keepdims=True)
    m_part = functools.reduce(lambda p, q: p + q, [msq[:, c : c + 128] for c in range(0, cblk, 128)])
    pl.semaphore_wait(barrier, n_row + n_col - 2)
    along_col(base, base_ss, base_rs)
    loads[3].wait()
    for im in range(images):
        a_s[PAD * im : PAD * im + positions, :] = act[im]
    loads[4].wait()
    poolg[...] = pool_ref[...] / positions
    loads[5].wait()

    def conv_columns(part):
        cols = pl.ds(pl.multiple_of(part * cblk, cblk), cblk)
        own_st = st.at[z, part]
        low = jnp.dot(a_s[...], w[:, cols], preferred_element_type=jnp.float32).astype(jnp.bfloat16)
        conv[:, cols] = low
        wide = low.astype(jnp.float32)
        total = jnp.sum(wide, axis=0, keepdims=True)
        mean = total / device_count
        own_st[0:1, :] = total
        own_st[1:2, :] = jnp.sum(wide * wide, axis=0, keepdims=True)
        up_sum = jnp.zeros((1, cblk), jnp.float32)
        upx_sum = jnp.zeros((1, cblk), jnp.float32)
        for im in range(images):
            rows = conv[PAD * im : PAD * im + positions, cols].astype(jnp.float32)
            keep = pre[im, :, cols].astype(jnp.float32) > 0
            pooled = poolg[im : im + 1, cols]
            up_sum += pooled * jnp.sum(jnp.where(keep, 1.0, 0.0), axis=0, keepdims=True)
            upx_sum += pooled * jnp.sum(jnp.where(keep, rows - mean, 0.0), axis=0, keepdims=True)
        own_st[2:3, :] = up_sum
        own_st[3:4, :] = upx_sum

    pl.loop(0, n_col)(conv_columns)
    stats = [
        send(st.at[z], st.at[z], st_ss.at[i - 1], st_rs.at[i - 1], r, col_peer(i)) for i in range(1, n_col)
    ]
    turned = a_s[...].T
    for q in range(n_row):
        at[q % 2, (q // 2) * rblk : (q // 2 + 1) * rblk, :] = turned[q * rblk : (q + 1) * rblk, :]
    for copy in stats:
        copy.wait_recv()
    base_out()
    parts = [jnp.concatenate([st[i, part] for part in range(n_col)], axis=1) for i in range(n_col)]
    mu = (parts[0][0:1] + parts[1][0:1] + parts[2][0:1] + parts[3][0:1]) / count
    square = parts[0][1:2] + parts[1][1:2] + parts[2][1:2] + parts[3][1:2]
    su = parts[0][2:3] + parts[1][2:3] + parts[2][2:3] + parts[3][2:3]
    rstd = lax.rsqrt(square / count - mu * mu + epsilon)
    sx = jnp.zeros_like(mu)
    for part in parts:
        sx += part[3:4] + (part[0:1] / device_count - mu) * part[2:3]
    sx = sx * rstd
    own_n1 = n1.at[r]
    own_n1[0:1, :out_chan] = sx
    own_n1[1:2, :out_chan] = su
    loads[6].wait()
    loads[7].wait()
    scale = bn_ref[0:1, :] * rstd
    coef[0:1, :] = scale
    coef[1:2, :] = scale * su / count
    coef[2:3, :] = scale * rstd * sx / count
    coef[3:4, :] = mu

    corner = 2 * y + x

    def quarter(s):
        i = 2 * (1 - s % 2) + 1 - s // 2
        p = 2 * flip(z // 2, 1 - s % 2) + flip(lax.rem(z, 2), 1 - s // 2)
        return i, p, p // 2

    def remote(src, dst, ss, rs, row, col):
        return pltpu.make_async_remote_copy(
            src_ref=src, dst_ref=dst, send_sem=ss, recv_sem=rs,
            device_id=(row, col), device_id_type=MESH,
        )

    def copy_a(s):
        return remote(sa.at[s], ra.at[s], a_ss.at[s], a_rs.at[s], sibling, z)

    def copy_b(s):
        return remote(sb.at[s], rb.at[s], b_ss.at[s], b_rs.at[s], plane_row(2, quarter(s)[2], k), z)

    def copy_c(s):
        return remote(sc.at[s], rc.at[s], c_ss.at[s], c_rs.at[s], plane_row(1, quarter(s)[2], k), z)

    def copy_d(s):
        i, p, _ = quarter(s)
        return remote(sd.at[s], rd.at[s], d_ss.at[s], d_rs.at[s], r, p)

    def stage_a(s):
        _, p, _ = quarter(s)
        cols = pl.ds(pl.multiple_of(p * cblk, cblk), cblk)
        scale_c, shift_c, slope_c, mu_c = (coef[n : n + 1, cols] for n in range(4))
        for im in range(images):
            span = slice(PAD * im, PAD * im + positions)
            rows = conv[span, cols].astype(jnp.float32)
            keep = pre[im, :, cols].astype(jnp.float32) > 0
            up = jnp.where(keep, scale_c * poolg[im : im + 1, cols], 0.0)
            cg[span, cols] = (up - shift_c - slope_c * (rows - mu_c)).astype(jnp.bfloat16)
        both = at[...].reshape(in_chan, images * PAD)
        product = jnp.dot(both, cg[:, cols], preferred_element_type=jnp.float32)
        own[s] = product.reshape(2, 4, rblk, cblk)
        sa[s] = own[s, 1 - k].astype(jnp.bfloat16)
        copy_a(s).start()

    def stage_b(s):
        _, _, h = quarter(s)
        copy_a(s).wait_recv()
        for j in range(2):
            q = (1 - h) * (2 * j + 1 - x) + h * (2 * (1 - y) + j)
            sb[s, j] = (own[s, k, q] + ra[s, q].astype(jnp.float32)).astype(jnp.bfloat16)
        copy_b(s).start()

    def stage_c(s):
        _, _, h = quarter(s)
        copy_b(s).wait_recv()
        j = (1 - h) * (1 - y) + h * (1 - x)
        q = (1 - h) * (2 * j + x) + h * (2 * y + j)
        sc[s] = (own[s, k, q] + ra[s, q].astype(jnp.float32) + rb[s, j].astype(jnp.float32)).astype(jnp.bfloat16)
        copy_c(s).start()

    def stage_d(s):
        _, _, h = quarter(s)
        copy_c(s).wait_recv()
        j = (1 - h) * y + h * x
        done = own[s, k, corner] + ra[s, corner].astype(jnp.float32) + rb[s, j].astype(jnp.float32) + rc[s].astype(jnp.float32)
        if isinstance(s, int) and s == 3:
            return done
        sd[s] = done.astype(jnp.bfloat16)
        copy_d(s).start()

    def input_rows(lo, hi):
        back = lax.dot_general(
            cg[PAD * lo : PAD * hi, :], w[...], (((1,), (1,)), ((), ())),
            preferred_element_type=jnp.float32,
        ).astype(jnp.bfloat16)
        for im in range(lo, hi):
            ig[im] = back[PAD * (im - lo) : PAD * (im - lo) + positions, :]

    @pl.loop(0, 4)
    def reduce_quarters(s):
        stage_a(s)
        pl.when(s >= 1)(lambda: stage_b(s - 1))
        pl.when(s >= 2)(lambda: stage_c(s - 2))

    stage_b(3)
    stage_d(0)
    input_rows(0, images // 2)
    stage_c(2)
    stage_d(1)
    base_relay()
    stage_c(3)
    input_rows(images // 2, images)
    put(ig, ig_hbm)
    stage_d(2)
    grad = stage_d(3)
    for i in range(n_col - 1):
        copy_d(i).wait_recv()
        grad += rd[i].astype(jnp.float32)
    grad = grad * (1.0 / total_images)

    gsq = jnp.sum(grad * grad, axis=0, keepdims=True)
    g_part = functools.reduce(lambda p, q: p + q, [gsq[:, c : c + 128] for c in range(0, cblk, 128)])
    own_n1[0:1, out_chan:] = g_part
    own_n1[1:2, out_chan:] = m_part
    norm1 = [
        send(n1.at[r], n1.at[r], n1_ss.at[j - 1], n1_rs.at[j - 1], row_peer(j), z) for j in range(1, n_row)
    ]
    gsum[block(r, z, cblk)] = grad.astype(jnp.bfloat16)
    along_col(gsum, gsum_ss, gsum_rs)
    grad_own_out(0)
    for copy in norm1:
        copy.wait_recv()
    all_sums = functools.reduce(lambda p, q: p + q, [n1[j] for j in range(n_row)])
    n2[z] = all_sums[:, out_chan:]
    norm2 = [
        send(n2.at[z], n2.at[z], n2_ss.at[i - 1], n2_rs.at[i - 1], r, col_peer(i)) for i in range(1, n_col)
    ]
    grad_own_out(1)
    sums = all_sums[:, :out_chan]
    new_bnv = momentum * bnv_ref[...] + learn_rate * (sums * (1.0 / total_images))
    nbv_ref[...] = new_bnv
    nbn_ref[...] = bn_ref[...] - new_bnv
    put(nbv_ref, nbv_hbm)
    put(nbn_ref, nbn_hbm)
    grad_near_out()
    for copy in norm2:
        copy.wait_recv()
    norm = functools.reduce(lambda p, q: p + q, [n2[i] for i in range(n_col)])
    gnorm = jnp.sqrt(jnp.sum(norm[0:1, :], axis=1, keepdims=True))
    wnorm = jnp.sqrt(jnp.sum(norm[1:2, :], axis=1, keepdims=True))
    trust = trust_coef * wnorm / (gnorm + weight_decay * wnorm)
    rate = learn_rate * trust
    weights_now = master_ref[...]
    new_velocity = momentum * velocity_ref[...] + rate * (grad + weight_decay * weights_now)
    nv_ref[...] = new_velocity
    nm_ref[...] = weights_now - new_velocity
    put(nv_ref, nv_hbm)
    put(nm_ref, nm_hbm)
    grad_far_out()

    def update(at_block):
        low = w[at_block].astype(jnp.float32)
        change = base[at_block].astype(jnp.float32)
        step = rate * (gsum[at_block].astype(jnp.float32) + weight_decay * low)
        nw_ref[at_block] = (low + (change - step)).astype(jnp.bfloat16)

    @pl.loop(0, 8)
    def update_own(e):
        update(block(2 * (e // 2) + k, e % 2, half))

    for n in range(4):
        base_piece(n, 7 + n, sibling, 1 - k).wait_recv()

    @pl.loop(0, 8)
    def update_other(e):
        n, t = e // 2, e % 2
        grad_piece(n, t, 10 + e, sibling, 1 - k).wait_recv()
        h = flip(z // 2, t)
        update(block(plane_row(n, h, 1 - k), h, half))

    put(nw_ref, nw_hbm)
    for copy in stats + norm1 + norm2 + sends:
        copy.wait_send()
    for s in range(4):
        copy_a(s).wait_send()
        copy_b(s).wait_send()
        copy_c(s).wait_send()
        if s < 3:
            copy_d(s).wait_send()
    for copy in puts:
        copy.wait()


def write_out(*refs):
    count = len(refs) // 3
    ins, outs, held = refs[:count], refs[count : 2 * count], refs[2 * count : 3 * count]
    in_sem, out_sem = refs[3 * count :]
    first = [pltpu.make_async_copy(ins[n], held[n], in_sem.at[n]) for n in range(count)]
    second = [pltpu.make_async_copy(held[n], outs[n], out_sem.at[n]) for n in range(count)]
    for copy in first:
        copy.start()
    for n in range(count):
        first[n].wait()
        second[n].start()
    for copy in second:
        copy.wait()


def fused(activations, pre_activation, pooled_grad, weights, master, velocity, bn_params, bn_velocity):
    images, positions, in_chan = activations.shape
    out_chan = weights.shape[1]
    rows = images * PAD
    rblk, cblk = master.shape
    f32, bf16 = jnp.float32, jnp.bfloat16
    hbm = pl.BlockSpec(memory_space=pltpu.HBM)
    dma = pltpu.SemaphoreType.DMA
    pairs = (3, 4, 4, 4, 3, 7, 3, 11, 18)
    flops = 6 * images * positions * in_chan * out_chan
    args = (activations, pre_activation, pooled_grad, weights, master, velocity, bn_params, bn_velocity)
    shapes = tuple(
        jax.ShapeDtypeStruct(a.shape, a.dtype)
        for a in (activations, master, master, weights, bn_params, bn_params)
    )
    results = pl.pallas_call(
        kernel,
        out_shape=shapes,
        in_specs=[hbm] * len(args),
        out_specs=(hbm,) * len(shapes),
        scratch_shapes=[pltpu.VMEM(a.shape, a.dtype) for a in args + shapes]
        + [
            pltpu.VMEM((rows, in_chan), bf16),
            pltpu.VMEM((2, in_chan // 2, rows), bf16),
            pltpu.VMEM((rows, out_chan), bf16),
            pltpu.VMEM((rows, out_chan), bf16),
            pltpu.VMEM(pooled_grad.shape, f32),
            pltpu.VMEM(weights.shape, bf16),
            pltpu.VMEM(weights.shape, bf16),
            pltpu.VMEM((4, 4, 4, cblk), f32),
            pltpu.VMEM((4, out_chan), f32),
            pltpu.VMEM((4, 4, rblk, cblk), bf16),
            pltpu.VMEM((4, 4, rblk, cblk), bf16),
            pltpu.VMEM((4, 2, 4, rblk, cblk), f32),
            pltpu.VMEM((4, 2, rblk, cblk), bf16),
            pltpu.VMEM((4, 2, rblk, cblk), bf16),
            pltpu.VMEM((4, rblk, cblk), bf16),
            pltpu.VMEM((4, rblk, cblk), bf16),
            pltpu.VMEM((3, rblk, cblk), bf16),
            pltpu.VMEM((3, rblk, cblk), bf16),
            pltpu.VMEM((8, 2, out_chan + 128), f32),
            pltpu.VMEM((4, 2, 128), f32),
            dma((8,)),
            dma((16,)),
        ]
        + [dma((n,)) for n in pairs for _ in range(2)],
        compiler_params=pltpu.CompilerParams(
            collective_id=0, has_side_effects=True, vmem_limit_bytes=LIMIT
        ),
        cost_estimate=pl.CostEstimate(flops=flops, bytes_accessed=8 * 1024 * 1024, transcendentals=0),
    )(*args)
    return pl.pallas_call(
        write_out,
        out_shape=shapes,
        in_specs=[hbm] * len(shapes),
        out_specs=(hbm,) * len(shapes),
        scratch_shapes=[pltpu.VMEM(a.shape, a.dtype) for a in shapes] + [dma((len(shapes),))] * 2,
        compiler_params=pltpu.CompilerParams(vmem_limit_bytes=LIMIT),
    )(*results)


def pick(mesh):
    if mesh.shape["row"] == 8 and mesh.shape["col"] == 4:
        return fused
    return body


def solution(mesh):
    placed = (
        P(("row", "col"), None, None),
        P(("row", "col"), None, None),
        P(("row", "col"), None),
        P(),
        P("row", "col"),
        P("row", "col"),
        P(),
        P(),
    )
    return jax.shard_map(
        pick(mesh),
        mesh=mesh,
        in_specs=placed,
        out_specs=(P(("row", "col"), None, None), P("row", "col"), P("row", "col"), P(), P(), P()),
        check_vma=False,
    )
```
